128 devices in a mesh: inst: 16 (over y, x_lo, core), tp: 8 (over x_hi, z).
Axes of the slice: x: 4 (x_hi: 2, x_lo: 2; x = x_hi * 2 + x_lo), y: 4, z: 4, core: 2. Of those that a mesh axis runs over, the one named last changes fastest.
Arguments:
- old_cache: bfloat16 [16384, 64, 256], P(('inst', 'tp')), may hold values from -6 to 6
- old_weight: bfloat16 [8192, 4096], P('tp'), may hold values from -4 to 4
- plan_src: int32 [128, 128], P(('inst', 'tp')), may hold values from 0 to 127, as said below
- plan_page: int32 [128, 128], P(('inst', 'tp')), may hold values from 0 to 127
- lengths: int32 [16, 2, 1], P('inst'), may hold values from 512 to 4096
- queries: bfloat16 [128, 4, 2048], P(('inst', 'tp')), may hold values from -100 to 100
- new_kv: bfloat16 [128, 4, 512], P(('inst', 'tp')), may hold values from -100 to 100
Outputs:
- layer_out: bfloat16 [128, 4, 4096], P(('inst', 'tp'))
- moved_cache: bfloat16 [16384, 64, 256], P(('inst', 'tp'))
The draws below stay inside these ranges and needn't reach their ends.
Inputs may be any that keep to these rules, and one draw needn't show every extreme that they name: `plan_src`: in every row at most 2 slots name the same source device, and some source is named by exactly 2 slots of that row.
All inputs are finite; a program needn't handle non-finite values.
Results may differ from the reference program's by a relative error of at most 0.011.
Values may be sent and summed in bfloat16 or wider, within the bound.
No kernel may reach another device: no remote copies, remote signals or barrier semaphores. Data moves between devices by JAX's collectives and lax.ppermute only.
A program may use at most 128 MiB of HBM per device.

```python
import jax
import jax.numpy as jnp
from jax import lax

QHEADS = 64
KVHEADS = 8
HEAD = 128
DW = 4096
LEN = 4096
PAGE = 64
REQ = 1
STEPS = 4
QDIM = 2048
PAGES = 128
N_INST = 16
N_TP = 8
DEVICES = 128


def plan_pair(key):
    devices_all = N_INST * N_TP
    capacity = 2 * PAGES // devices_all
    row_keys = jax.random.split(key, devices_all)

    def one_row(row_key):
        key_order, key_count, key_spread, key_page = jax.random.split(row_key, 4)
        shuffle = jax.random.permutation(key_order, jnp.arange(devices_all, dtype=jnp.int32))
        counts = jax.random.randint(key_count, (devices_all,), capacity // 2, capacity + 1).astype(jnp.int32)
        counts = counts.at[0].set(capacity)
        bounds = jnp.cumsum(counts)
        slot_ids = jnp.arange(PAGES, dtype=jnp.int32)
        owner = jnp.sum((bounds[None, :] <= slot_ids[:, None]).astype(jnp.int32), axis=1)
        sources = shuffle[owner]
        spread = jax.random.permutation(key_spread, jnp.arange(PAGES, dtype=jnp.int32))
        sources = sources[spread]
        source_page = jax.random.randint(key_page, (PAGES,), 0, PAGES).astype(jnp.int32)
        return (sources.astype(jnp.int32), source_page)
    return jax.vmap(one_row)(row_keys)


def draw_plan_src(key, part):
    sources, source_page = plan_pair(key)
    return sources


def draw_plan_page(key, part):
    sources, source_page = plan_pair(key)
    return source_page


def query_base(key):
    return jax.random.normal(key, (N_INST * N_TP * REQ, STEPS, QDIM), jnp.float32)


def draw_queries(key, part):
    base_draw = query_base(key)
    return base_draw.astype(jnp.bfloat16)


def draw_new_kv(key, part):
    key = jax.random.fold_in(key, 7)
    row_count = N_INST * N_TP * REQ
    kv_local = 2 * KVHEADS // N_TP
    fresh_rows = jax.random.normal(key, (row_count, STEPS, kv_local * 2 * HEAD), jnp.float32)
    return fresh_rows.astype(jnp.bfloat16)


def set_ends(entries, own_key, low, high):
    shape = entries.shape
    place = [jax.random.randint(jax.random.fold_in(own_key, axis), (), 0, shape[axis]) for axis in range(len(shape))]
    entries = entries.at[tuple(place)].set(low)
    longest = shape.index(max(shape))
    place[longest] = (place[longest] + 1) % shape[longest]
    return entries.at[tuple(place)].set(high)


def block_levels(own_key, extent, cuts, low, largest):
    loudness, own = 1.0, jax.random.fold_in(own_key, 6)
    for dim, parts in cuts:
        draws = jnp.exp(jax.random.uniform(jax.random.fold_in(own, dim), (parts,), jnp.float32, low / len(cuts), largest / len(cuts)))
        loudness = loudness * jnp.repeat(draws, extent[dim] // parts).reshape([-1 if axis == dim else 1 for axis in range(len(extent))])
    return loudness


def gaussian(own_key, dims, deviation, most, pieces=(), kind=jnp.bfloat16):
    level = block_levels(own_key, dims, pieces, -0.22, 0.18) if pieces else 1.0
    values = jax.random.normal(own_key, dims, jnp.float32) * deviation * level
    return jnp.minimum(jnp.maximum(values, -most), most).astype(kind)


def setup_inputs(seed: int = 0) -> dict:
    splits = jax.random.split(jax.random.key(seed), 8)
    old_cache = gaussian(splits[0], (DEVICES * PAGES, PAGE, 2 * HEAD), 1.0, 6.0, ((0, 128),))
    old_weight = gaussian(splits[1], (QHEADS * HEAD, DW), (QHEADS * HEAD // LEN) ** -0.5, 4.0, ((0, 8),))
    plan_src = draw_plan_src(jax.random.fold_in(splits[7], 71), 0)
    plan_page = draw_plan_page(jax.random.fold_in(splits[7], 71), 0)
    lengths = set_ends(jax.random.randint(splits[4], (N_INST, 2, REQ), LEN // 8, LEN + 1), jax.random.fold_in(splits[4], 1), LEN // 8, LEN).astype(jnp.int32)
    queries = draw_queries(jax.random.fold_in(splits[7], 71), 0)
    new_kv = draw_new_kv(jax.random.fold_in(splits[7], 71), 0)
    return dict(old_cache=old_cache, old_weight=old_weight, plan_src=plan_src, plan_page=plan_page, lengths=lengths, queries=queries, new_kv=new_kv)


def attend(cache, queries, new_kv, lengths_own):
    requests, steps, q_width = queries.shape
    kv_local = cache.shape[1]
    head = cache.shape[3] // 2
    groups = q_width // (kv_local * head)
    query_rows = queries.astype(jnp.float32).reshape(requests, steps, kv_local, groups, head)
    key_rows = cache[..., :head].astype(jnp.float32)
    value_rows = cache[..., head:].astype(jnp.float32)
    fresh_rows = new_kv.astype(jnp.float32).reshape(requests, steps, kv_local, 2 * head)
    fresh_keys = fresh_rows[..., :head]
    fresh_values = fresh_rows[..., head:]
    score_scale = head ** -0.5
    cache_scores = jnp.einsum('rtkgd,rkld->rkgtl', query_rows, key_rows) * score_scale
    positions = jnp.arange(cache.shape[2], dtype=jnp.int32)
    visible = positions[None, :] < lengths_own[:, None]
    cache_scores = jnp.where(visible[:, None, None, None, :], cache_scores, jnp.float32(-1e30))
    fresh_scores = jnp.einsum('rtkgd,rukd->rkgtu', query_rows, fresh_keys) * score_scale
    causal = jnp.arange(steps)[:, None] >= jnp.arange(steps)[None, :]
    fresh_scores = jnp.where(causal, fresh_scores, jnp.float32(-1e30))
    highest = jnp.maximum(jnp.max(cache_scores, axis=-1), jnp.max(fresh_scores, axis=-1))
    cache_exp = jnp.exp(cache_scores - highest[..., None])
    fresh_exp = jnp.exp(fresh_scores - highest[..., None])
    summed = jnp.sum(cache_exp, axis=-1) + jnp.sum(fresh_exp, axis=-1)
    cache_prob = (cache_exp / summed[..., None]).astype(jnp.bfloat16).astype(jnp.float32)
    fresh_prob = (fresh_exp / summed[..., None]).astype(jnp.bfloat16).astype(jnp.float32)
    mixed = jnp.einsum('rkgtl,rkld->rtkgd', cache_prob, value_rows)
    mixed = mixed + jnp.einsum('rkgtu,rukd->rtkgd', fresh_prob, fresh_values)
    return mixed.reshape(requests * steps, q_width).astype(jnp.bfloat16)


def reference(old_cache, old_weight, plan_src, plan_page, lengths, queries, new_kv):
    devices_all = N_INST * N_TP
    page_count = plan_src.shape[1]
    kv_local = 2 * KVHEADS // N_TP
    q_width = queries.shape[2]
    flat_index = (plan_src * page_count + plan_page).reshape(-1).astype(jnp.int32)
    moved_cache = old_cache[flat_index]
    per_device = moved_cache.reshape(devices_all, REQ, kv_local, LEN, 2 * HEAD)

    def one_device(device):
        cache = lax.dynamic_index_in_dim(per_device, device, 0, keepdims=False)
        tp_index = device % N_TP
        weight = lax.dynamic_slice_in_dim(old_weight, (tp_index // 2) * q_width, q_width, 0)
        lengths_own = lengths[device // N_TP, tp_index % 2]
        own_queries = lax.dynamic_slice_in_dim(queries, device * REQ, REQ, 0)
        own_kv = lax.dynamic_slice_in_dim(new_kv, device * REQ, REQ, 0)
        mixed = attend(cache, own_queries, own_kv, lengths_own)
        return jnp.dot(mixed, weight, preferred_element_type=jnp.float32).reshape(REQ, STEPS, DW)

    partials = lax.map(one_device, jnp.arange(devices_all, dtype=jnp.int32))
    grouped = jnp.sum(partials.reshape(N_INST, N_TP // 2, 2, REQ, STEPS, DW), axis=1)
    spread = jnp.broadcast_to(grouped[:, None], (N_INST, N_TP // 2, 2, REQ, STEPS, DW))
    layer_out = spread.reshape(devices_all * REQ, STEPS, DW).astype(jnp.bfloat16)
    return (layer_out, moved_cache)
```

```python
import functools

import jax
import jax.numpy as jnp
from jax import lax
from jax.experimental import pallas as pl
from jax.experimental.pallas import tpu as pltpu
from jax.sharding import PartitionSpec as P

BOTH = ("inst", "tp")
ANY = pl.BlockSpec(memory_space=pl.ANY)
VMEM = pl.BlockSpec(memory_space=pltpu.VMEM)
SMEM = pl.BlockSpec(memory_space=pltpu.SMEM)
LIMIT = 48 * 1024 * 1024


def flipped(value, bits):
    size = lax.axis_size("tp")
    return lax.ppermute(value, "tp", [(i, i ^ bits) for i in range(size)])


def plan_kernel(src_ref, page_ref, wanted_ref, place_ref):
    slots = src_ref.shape[1]
    sources = wanted_ref.shape[0]
    src = src_ref[...]
    order = lax.broadcasted_iota(jnp.int32, (1, slots), 1)
    coded = order * 65536 + page_ref[...]
    named = lax.broadcasted_iota(jnp.int32, (sources, slots), 0) == src
    first = jnp.min(jnp.where(named, coded, slots * 65536), axis=1, keepdims=True)
    last = jnp.max(jnp.where(named, coded, 0), axis=1, keepdims=True)
    found = first < slots * 65536
    wanted_ref[:, 0:1] = jnp.where(found, first & 65535, 0)
    wanted_ref[:, 1:2] = jnp.where(found, last & 65535, 0)
    rows = lax.broadcasted_iota(jnp.int32, (slots, slots), 0)
    columns = lax.broadcasted_iota(jnp.int32, (slots, slots), 1)
    src_column = jnp.max(jnp.where(rows == columns, src, 0), axis=1, keepdims=True)
    again = jnp.max(jnp.where((src_column == src) & (rows < columns), 1, 0), axis=0, keepdims=True)
    place_ref[...] = src * 2 + again


def make_plan(plan_src, plan_page, sources):
    slots = plan_src.shape[1]
    return pl.pallas_call(
        plan_kernel,
        out_shape=(
            jax.ShapeDtypeStruct((sources, 2), jnp.int32),
            jax.ShapeDtypeStruct((1, slots), jnp.int32),
        ),
        in_specs=[VMEM, VMEM],
        out_specs=(VMEM, VMEM),
        name="make_plan",
    )(plan_src, plan_page)


def take_kernel(at_ref, from_ref, to_ref, sem):
    columns = at_ref.shape[1]

    @pl.loop(0, at_ref.shape[0])
    def _(row):
        for column in range(columns):
            pltpu.make_async_copy(
                from_ref.at[at_ref[row, column]], to_ref.at[row * columns + column], sem
            ).start()

    pltpu.make_async_copy(to_ref, to_ref, sem).wait()


def take(pages, at, name):
    count = at.shape[0] * at.shape[1]
    shape = (count,) + pages.shape[1:]
    return pl.pallas_call(
        take_kernel,
        out_shape=jax.ShapeDtypeStruct(shape, pages.dtype),
        in_specs=[SMEM, ANY],
        out_specs=ANY,
        scratch_shapes=[pltpu.SemaphoreType.DMA],
        cost_estimate=pl.CostEstimate(
            flops=0, bytes_accessed=2 * count * pages.shape[1] * pages.shape[2] * 2, transcendentals=0
        ),
        name=name,
    )(at, pages)


def attend_kernel(info_ref, place_ref, pages_ref, query_ref, fresh_ref, out_ref, cache, sem):
    half, page, width = cache.shape
    head = width // 2
    which = info_ref[0]
    length = info_ref[1]

    @pl.loop(0, half)
    def _(slot):
        pltpu.make_async_copy(
            pages_ref.at[place_ref[0, which * half + slot]], cache.at[slot], sem
        ).start()

    query = query_ref[which]
    steps = fresh_ref.shape[1]
    rows = query.shape[0]
    scale = head ** (-0.5)
    contract_last = (((1,), (1,)), ((), ()))
    fresh = fresh_ref[which]
    fresh_scores = (
        lax.dot_general(query, fresh[:, :head], contract_last, preferred_element_type=jnp.float32) * scale
    )
    step_of = lax.broadcasted_iota(jnp.int32, (rows, steps), 0) // (rows // steps)
    key_step = lax.broadcasted_iota(jnp.int32, (rows, steps), 1)
    fresh_scores = jnp.where(step_of >= key_step, fresh_scores, jnp.float32(-1e30))
    pltpu.make_async_copy(cache, cache, sem).wait()
    keys = cache[:, :, :head].reshape(half * page, head)
    scores = lax.dot_general(query, keys, contract_last, preferred_element_type=jnp.float32) * scale
    position = lax.broadcasted_iota(jnp.int32, scores.shape, 1)
    scores = jnp.where(position < length, scores, jnp.float32(-1e30))
    highest = jnp.maximum(
        jnp.max(scores, axis=1, keepdims=True), jnp.max(fresh_scores, axis=1, keepdims=True)
    )
    weights = jnp.exp(scores - highest)
    fresh_weights = jnp.exp(fresh_scores - highest)
    total = jnp.sum(weights, axis=1, keepdims=True) + jnp.sum(fresh_weights, axis=1, keepdims=True)
    values = cache[:, :, head:].reshape(half * page, head)
    mixed = jnp.dot((weights / total).astype(jnp.bfloat16), values, preferred_element_type=jnp.float32)
    fresh_prob = (fresh_weights / total).astype(jnp.bfloat16).astype(jnp.float32)
    fresh_values = fresh[:, head:].astype(jnp.float32)
    for step in range(steps):
        mixed = mixed + fresh_prob[:, step : step + 1] * fresh_values[step : step + 1, :]
    out_ref[...] = mixed.astype(jnp.bfloat16)


def attend(which, length, place, arrived, queries, fresh, name):
    half = place.shape[1] // 2
    rows, head = queries.shape[1:]
    info = jnp.stack([which, length]).astype(jnp.int32)
    return pl.pallas_call(
        attend_kernel,
        out_shape=jax.ShapeDtypeStruct((rows, head), jnp.bfloat16),
        in_specs=[SMEM, SMEM, ANY, VMEM, VMEM],
        out_specs=VMEM,
        scratch_shapes=[
            pltpu.VMEM((half,) + arrived.shape[1:], arrived.dtype),
            pltpu.SemaphoreType.DMA,
        ],
        compiler_params=pltpu.CompilerParams(vmem_limit_bytes=LIMIT),
        cost_estimate=pl.CostEstimate(
            flops=4 * rows * half * arrived.shape[1] * head,
            bytes_accessed=half * arrived.shape[1] * arrived.shape[2] * 2,
            transcendentals=rows * half * arrived.shape[1],
        ),
        name=name,
    )(info, place, arrived, queries, fresh)


def on_device(old_cache, old_weight, plan_src, plan_page, lengths, queries, new_kv):
    devices = lax.axis_size("inst") * lax.axis_size("tp")
    steps = queries.shape[1]
    width = old_cache.shape[2]
    heads = new_kv.shape[2] // width
    head = width // 2
    groups = queries.shape[2] // (heads * head)
    side = lax.axis_index("tp") % 2

    wanted, place = make_plan(plan_src, plan_page, devices)
    asked = lax.all_to_all(wanted, BOTH, split_axis=0, concat_axis=0, tiled=True)
    outgoing = take(old_cache, asked, "take_outgoing")
    outgoing = outgoing.reshape((devices, 2) + old_cache.shape[1:])
    arrived = lax.all_to_all(outgoing, BOTH, split_axis=0, concat_axis=0, tiled=True)
    arrived = arrived.reshape((devices * 2,) + old_cache.shape[1:])

    rows = queries.reshape(steps, heads, groups, head).transpose(1, 0, 2, 3)
    rows = rows.reshape(heads, steps * groups, head)
    fresh = new_kv.reshape(steps, heads, width).transpose(1, 0, 2)
    length = lax.dynamic_index_in_dim(lengths[0, :, 0], side, 0, keepdims=False)
    passed = attend(1 - side, length, place, arrived, rows, fresh, "attend_other")
    partner = flipped(passed, 1)
    kept = attend(side, length, place, arrived, rows, fresh, "attend_own")
    moved = take(arrived, place.reshape(-1, 1), "take_arrived")

    both = jnp.stack([kept, partner]).reshape(2 * steps, groups * head)
    partial = jnp.dot(both, old_weight, preferred_element_type=jnp.float32)
    own, other = partial[:steps], partial[steps:]
    own = own + flipped(other.astype(jnp.bfloat16), 1).astype(jnp.float32)
    sent = own.astype(jnp.bfloat16)
    parts = [flipped(sent, bits) for bits in range(2, lax.axis_size("tp"), 2)]
    for part in parts:
        own = own + part.astype(jnp.float32)
    return own.reshape(1, steps, -1).astype(jnp.bfloat16), moved


def solution(mesh):
    placed = (
        P(BOTH, None, None),
        P("tp", None),
        P(BOTH, None),
        P(BOTH, None),
        P("inst", None, None),
        P(BOTH, None, None),
        P(BOTH, None, None),
    )
    return jax.shard_map(
        on_device,
        mesh=mesh,
        in_specs=placed,
        out_specs=(P(BOTH, None, None), P(BOTH, None, None)),
        check_vma=False,
    )
```

```python
import functools

import jax
import jax.numpy as jnp
from jax import lax
from jax.experimental import pallas as pl
from jax.experimental.pallas import tpu as pltpu
from jax.sharding import PartitionSpec as P

BOTH = ("inst", "tp")
ANY = pl.BlockSpec(memory_space=pl.ANY)
VMEM = pl.BlockSpec(memory_space=pltpu.VMEM)
SMEM = pl.BlockSpec(memory_space=pltpu.SMEM)
LIMIT = 24 * 1024 * 1024


def flipped(value, bits):
    size = lax.axis_size("tp")
    return lax.ppermute(value, "tp", [(i, i ^ bits) for i in range(size)])


def plan_kernel(src_ref, page_ref, wanted_ref, place_ref):
    slots = src_ref.shape[1]
    sources = wanted_ref.shape[0]
    src = src_ref[...]
    order = lax.broadcasted_iota(jnp.int32, (1, slots), 1)
    coded = order * 65536 + page_ref[...]
    named = lax.broadcasted_iota(jnp.int32, (sources, slots), 0) == src
    first = jnp.min(jnp.where(named, coded, slots * 65536), axis=1, keepdims=True)
    last = jnp.max(jnp.where(named, coded, 0), axis=1, keepdims=True)
    found = first < slots * 65536
    wanted_ref[:, 0:1] = jnp.where(found, first & 65535, 0)
    wanted_ref[:, 1:2] = jnp.where(found, last & 65535, 0)
    rows = lax.broadcasted_iota(jnp.int32, (slots, slots), 0)
    columns = lax.broadcasted_iota(jnp.int32, (slots, slots), 1)
    src_column = jnp.max(jnp.where(rows == columns, src, 0), axis=1, keepdims=True)
    again = jnp.max(jnp.where((src_column == src) & (rows < columns), 1, 0), axis=0, keepdims=True)
    place_ref[...] = src * 2 + again


def make_plan(plan_src, plan_page, sources):
    slots = plan_src.shape[1]
    return pl.pallas_call(
        plan_kernel,
        out_shape=(
            jax.ShapeDtypeStruct((sources, 2), jnp.int32),
            jax.ShapeDtypeStruct((1, slots), jnp.int32),
        ),
        in_specs=[VMEM, VMEM],
        out_specs=(VMEM, VMEM),
        name="make_plan",
    )(plan_src, plan_page)


def take_kernel(at_ref, from_ref, to_ref, sem):
    columns = at_ref.shape[1]

    @pl.loop(0, at_ref.shape[0], unroll=4)
    def _(row):
        for column in range(columns):
            pltpu.make_async_copy(
                from_ref.at[at_ref[row, column]], to_ref.at[row * columns + column], sem
            ).start()

    pltpu.make_async_copy(to_ref, to_ref, sem).wait()


def take(pages, at):
    count = at.shape[0] * at.shape[1]
    shape = (count,) + pages.shape[1:]
    return pl.pallas_call(
        take_kernel,
        out_shape=jax.ShapeDtypeStruct(shape, pages.dtype),
        in_specs=[SMEM, VMEM],
        out_specs=ANY,
        scratch_shapes=[pltpu.SemaphoreType.DMA],
        compiler_params=pltpu.CompilerParams(vmem_limit_bytes=LIMIT),
        cost_estimate=pl.CostEstimate(
            flops=0, bytes_accessed=2 * count * pages.shape[1] * pages.shape[2] * 2, transcendentals=0
        ),
        name="take_outgoing",
    )(at, pltpu.with_memory_space_constraint(pages, pltpu.VMEM))


def attend_kernel(info_ref, place_ref, pages_ref, query_ref, fresh_ref, *rest):
    out_ref, moved_ref, cache, sem, out_sem = rest[-5:]
    half, page, width = cache.shape
    head = width // 2
    which = info_ref[0]
    length = info_ref[1]

    @pl.loop(0, half, unroll=4)
    def _(slot):
        pltpu.make_async_copy(
            pages_ref.at[place_ref[0, which * half + slot]], cache.at[slot], sem
        ).start()

    query = query_ref[which]
    steps = fresh_ref.shape[1]
    rows = query.shape[0]
    scale = head ** (-0.5)
    contract_last = (((1,), (1,)), ((), ()))
    fresh = fresh_ref[which]
    fresh_scores = (
        lax.dot_general(query, fresh[:, :head], contract_last, preferred_element_type=jnp.float32) * scale
    )
    step_of = lax.broadcasted_iota(jnp.int32, (rows, steps), 0) % steps
    key_step = lax.broadcasted_iota(jnp.int32, (rows, steps), 1)
    fresh_scores = jnp.where(step_of >= key_step, fresh_scores, jnp.float32(-1e30))
    pltpu.make_async_copy(cache, cache, sem).wait()
    store = pltpu.make_async_copy(cache, moved_ref.at[pl.ds(which * half, half)], out_sem)
    store.start()
    keys = cache[:, :, :head].reshape(half * page, head)
    scores = lax.dot_general(query, keys, contract_last, preferred_element_type=jnp.float32) * scale
    position = lax.broadcasted_iota(jnp.int32, scores.shape, 1)
    scores = jnp.where(position < length, scores, jnp.float32(-1e30))
    highest = jnp.maximum(
        jnp.max(scores, axis=1, keepdims=True), jnp.max(fresh_scores, axis=1, keepdims=True)
    )
    weights = jnp.exp(scores - highest)
    fresh_weights = jnp.exp(fresh_scores - highest)
    total = jnp.sum(weights, axis=1, keepdims=True) + jnp.sum(fresh_weights, axis=1, keepdims=True)
    values = cache[:, :, head:].reshape(half * page, head)
    mixed = jnp.dot((weights / total).astype(jnp.bfloat16), values, preferred_element_type=jnp.float32)
    fresh_prob = (fresh_weights / total).astype(jnp.bfloat16).astype(jnp.float32)
    fresh_values = fresh[:, head:].astype(jnp.float32)
    for step in range(steps):
        mixed = mixed + fresh_prob[:, step : step + 1] * fresh_values[step : step + 1, :]
    out_ref[...] = mixed.astype(jnp.bfloat16)
    store.wait()


def attend(which, length, place, arrived, queries, fresh, moved, name):
    half = place.shape[1] // 2
    rows, head = queries.shape[1:]
    info = jnp.stack([which, length]).astype(jnp.int32)
    begun = [] if moved is None else [moved]
    return pl.pallas_call(
        attend_kernel,
        out_shape=(
            jax.ShapeDtypeStruct((rows, head), jnp.bfloat16),
            jax.ShapeDtypeStruct((2 * half,) + arrived.shape[1:], arrived.dtype),
        ),
        in_specs=[SMEM, SMEM, ANY, VMEM, VMEM] + [ANY for _ in begun],
        out_specs=(VMEM, ANY),
        input_output_aliases={5: 1} if begun else {},
        scratch_shapes=[
            pltpu.VMEM((half,) + arrived.shape[1:], arrived.dtype),
            pltpu.SemaphoreType.DMA,
            pltpu.SemaphoreType.DMA,
        ],
        compiler_params=pltpu.CompilerParams(vmem_limit_bytes=LIMIT),
        cost_estimate=pl.CostEstimate(
            flops=4 * rows * half * arrived.shape[1] * head,
            bytes_accessed=2 * half * arrived.shape[1] * arrived.shape[2] * 2,
            transcendentals=rows * half * arrived.shape[1],
        ),
        name=name,
    )(info, place, arrived, queries, fresh, *begun)


def project_kernel(kept_ref, partner_ref, weight_ref, own_ref, other_ref):
    steps = own_ref.shape[0]
    rows = []
    for ref in (kept_ref, partner_ref):
        value = ref[...].astype(jnp.float32)
        rows.append(
            jnp.concatenate([value[at : at + steps] for at in range(0, value.shape[0], steps)], axis=1)
        )
    both = jnp.concatenate(rows, axis=0).astype(jnp.bfloat16)
    tile = 1024
    for at in range(0, weight_ref.shape[1], tile):
        product = jnp.dot(both, weight_ref[:, at : at + tile], preferred_element_type=jnp.float32)
        own_ref[:, at : at + tile] = product[:steps]
        other_ref[:, at : at + tile] = product[steps:].astype(jnp.bfloat16)


def project(kept, partner, weight, steps):
    wide = weight.shape[1]
    return pl.pallas_call(
        project_kernel,
        out_shape=(
            jax.ShapeDtypeStruct((steps, wide), jnp.float32),
            jax.ShapeDtypeStruct((steps, wide), jnp.bfloat16),
        ),
        in_specs=[VMEM, VMEM, VMEM],
        out_specs=(VMEM, VMEM),
        compiler_params=pltpu.CompilerParams(vmem_limit_bytes=LIMIT),
        cost_estimate=pl.CostEstimate(
            flops=4 * steps * weight.size, bytes_accessed=weight.size * 2, transcendentals=0
        ),
        name="project",
    )(kept, partner, pltpu.with_memory_space_constraint(weight, pltpu.VMEM))


def on_device(old_cache, old_weight, plan_src, plan_page, lengths, queries, new_kv):
    devices = lax.axis_size("inst") * lax.axis_size("tp")
    steps = queries.shape[1]
    width = old_cache.shape[2]
    heads = new_kv.shape[2] // width
    head = width // 2
    groups = queries.shape[2] // (heads * head)
    side = lax.axis_index("tp") % 2

    wanted, place = make_plan(plan_src, plan_page, devices)
    asked = lax.all_to_all(wanted, BOTH, split_axis=0, concat_axis=0, tiled=True)
    outgoing = take(old_cache, asked)
    outgoing = outgoing.reshape((devices, 2) + old_cache.shape[1:])
    arrived = lax.all_to_all(outgoing, BOTH, split_axis=0, concat_axis=0, tiled=True)
    arrived = arrived.reshape((devices * 2,) + old_cache.shape[1:])

    rows = queries.reshape(steps, heads, groups, head).transpose(1, 2, 0, 3)
    rows = rows.reshape(heads, groups * steps, head)
    fresh = new_kv.reshape(steps, heads, width).transpose(1, 0, 2)
    length = lax.dynamic_index_in_dim(lengths[0, :, 0], side, 0, keepdims=False)
    passed, moved = attend(1 - side, length, place, arrived, rows, fresh, None, "attend_other")
    partner = flipped(passed, 1)
    kept, moved = attend(side, length, place, arrived, rows, fresh, moved, "attend_own")

    own, other = project(kept, partner, old_weight, steps)
    own = own + flipped(other, 1).astype(jnp.float32)
    sent = own.astype(jnp.bfloat16)
    parts = [flipped(sent, bits) for bits in range(2, lax.axis_size("tp"), 2)]
    for part in parts:
        own = own + part.astype(jnp.float32)
    return own.reshape(1, steps, -1).astype(jnp.bfloat16), moved


def solution(mesh):
    placed = (
        P(BOTH, None, None),
        P("tp", None),
        P(BOTH, None),
        P(BOTH, None),
        P("inst", None, None),
        P(BOTH, None, None),
        P(BOTH, None, None),
    )
    return jax.shard_map(
        on_device,
        mesh=mesh,
        in_specs=placed,
        out_specs=(P(BOTH, None, None), P(BOTH, None, None)),
        check_vma=False,
    )
```

```python
import functools

import jax
import jax.numpy as jnp
from jax import lax
from jax.experimental import pallas as pl
from jax.experimental.pallas import tpu as pltpu
from jax.sharding import PartitionSpec as P

BOTH = ("inst", "tp")
HBM = pl.BlockSpec(memory_space=pltpu.HBM)
VMEM = pl.BlockSpec(memory_space=pltpu.VMEM)
SMEM = pl.BlockSpec(memory_space=pltpu.SMEM)
LIMIT = 24 * 1024 * 1024


def flipped(value, bits):
    size = lax.axis_size("tp")
    return lax.ppermute(value, "tp", [(i, i ^ bits) for i in range(size)])


def plan_kernel(src_ref, page_ref, cache_ref, wanted_ref, place_ref, held_ref, sem):
    hold = pltpu.make_async_copy(cache_ref, held_ref, sem)
    hold.start()
    slots = src_ref.shape[1]
    sources = wanted_ref.shape[0]
    src = src_ref[...]
    order = lax.broadcasted_iota(jnp.int32, (1, slots), 1)
    coded = order * 65536 + page_ref[...]
    named = lax.broadcasted_iota(jnp.int32, (sources, slots), 0) == src
    first = jnp.min(jnp.where(named, coded, slots * 65536), axis=1, keepdims=True)
    last = jnp.max(jnp.where(named, coded, 0), axis=1, keepdims=True)
    found = first < slots * 65536
    wanted_ref[:, 0:1] = jnp.where(found, first & 65535, 0)
    wanted_ref[:, 1:2] = jnp.where(found, last & 65535, 0)
    rows = lax.broadcasted_iota(jnp.int32, (slots, slots), 0)
    columns = lax.broadcasted_iota(jnp.int32, (slots, slots), 1)
    src_column = jnp.max(jnp.where(rows == columns, src, 0), axis=1, keepdims=True)
    again = jnp.max(jnp.where((src_column == src) & (rows < columns), 1, 0), axis=0, keepdims=True)
    place_ref[...] = src * 2 + again
    hold.wait()


def make_plan(plan_src, plan_page, pages, sources):
    slots = plan_src.shape[1]
    return pl.pallas_call(
        plan_kernel,
        out_shape=(
            jax.ShapeDtypeStruct((sources, 2), jnp.int32),
            jax.ShapeDtypeStruct((1, slots), jnp.int32),
            pltpu.VMEM(pages.shape, pages.dtype),
        ),
        in_specs=[VMEM, VMEM, HBM],
        out_specs=(VMEM, VMEM, VMEM),
        scratch_shapes=[pltpu.SemaphoreType.DMA],
        compiler_params=pltpu.CompilerParams(vmem_limit_bytes=LIMIT),
        name="make_plan",
    )(plan_src, plan_page, pltpu.with_memory_space_constraint(pages, pltpu.HBM))


def take_kernel(at_ref, from_ref, to_ref, sem):
    columns = at_ref.shape[1]

    @pl.loop(0, at_ref.shape[0], unroll=4)
    def _(row):
        for column in range(columns):
            pltpu.make_async_copy(
                from_ref.at[at_ref[row, column]], to_ref.at[row * columns + column], sem
            ).start()

    pltpu.make_async_copy(to_ref, to_ref, sem).wait()


def take(pages, at):
    count = at.shape[0] * at.shape[1]
    shape = (count,) + pages.shape[1:]
    return pl.pallas_call(
        take_kernel,
        out_shape=pltpu.HBM(shape, pages.dtype),
        in_specs=[SMEM, VMEM],
        out_specs=HBM,
        scratch_shapes=[pltpu.SemaphoreType.DMA],
        compiler_params=pltpu.CompilerParams(vmem_limit_bytes=LIMIT),
        cost_estimate=pl.CostEstimate(
            flops=0, bytes_accessed=2 * count * pages.shape[1] * pages.shape[2] * 2, transcendentals=0
        ),
        name="take_outgoing",
    )(at, pltpu.with_memory_space_constraint(pages, pltpu.VMEM))


def attend_kernel(info_ref, place_ref, pages_ref, query_ref, fresh_ref, *rest):
    out_ref, moved_ref, cache, sem, out_sem = rest[-5:]
    half, page, width = cache.shape
    head = width // 2
    which = info_ref[0]
    length = info_ref[1]

    @pl.loop(0, half, unroll=4)
    def _(slot):
        pltpu.make_async_copy(
            pages_ref.at[place_ref[0, which * half + slot]], cache.at[slot], sem
        ).start()

    query = query_ref[which]
    steps = fresh_ref.shape[1]
    rows = query.shape[0]
    scale = head ** (-0.5)
    contract_last = (((1,), (1,)), ((), ()))
    fresh = fresh_ref[which]
    fresh_scores = (
        lax.dot_general(query, fresh[:, :head], contract_last, preferred_element_type=jnp.float32) * scale
    )
    step_of = lax.broadcasted_iota(jnp.int32, (rows, steps), 0) % steps
    key_step = lax.broadcasted_iota(jnp.int32, (rows, steps), 1)
    fresh_scores = jnp.where(step_of >= key_step, fresh_scores, jnp.float32(-1e30))
    pltpu.make_async_copy(cache, cache, sem).wait()
    store = pltpu.make_async_copy(cache, moved_ref.at[pl.ds(which * half, half)], out_sem)
    store.start()
    keys = cache[:, :, :head].reshape(half * page, head)
    scores = lax.dot_general(query, keys, contract_last, preferred_element_type=jnp.float32) * scale
    position = lax.broadcasted_iota(jnp.int32, scores.shape, 1)
    scores = jnp.where(position < length, scores, jnp.float32(-1e30))
    highest = jnp.maximum(
        jnp.max(scores, axis=1, keepdims=True), jnp.max(fresh_scores, axis=1, keepdims=True)
    )
    weights = jnp.exp(scores - highest)
    fresh_weights = jnp.exp(fresh_scores - highest)
    total = jnp.sum(weights, axis=1, keepdims=True) + jnp.sum(fresh_weights, axis=1, keepdims=True)
    values = cache[:, :, head:].reshape(half * page, head)
    mixed = jnp.dot((weights / total).astype(jnp.bfloat16), values, preferred_element_type=jnp.float32)
    fresh_prob = (fresh_weights / total).astype(jnp.bfloat16).astype(jnp.float32)
    fresh_values = fresh[:, head:].astype(jnp.float32)
    for step in range(steps):
        mixed = mixed + fresh_prob[:, step : step + 1] * fresh_values[step : step + 1, :]
    out_ref[...] = mixed.astype(jnp.bfloat16)
    store.wait()


def attend(which, length, place, arrived, queries, fresh, moved, name):
    half = place.shape[1] // 2
    rows, head = queries.shape[1:]
    info = jnp.stack([which, length]).astype(jnp.int32)
    begun = [] if moved is None else [moved]
    return pl.pallas_call(
        attend_kernel,
        out_shape=(
            jax.ShapeDtypeStruct((rows, head), jnp.bfloat16),
            jax.ShapeDtypeStruct((2 * half,) + arrived.shape[1:], arrived.dtype),
        ),
        in_specs=[SMEM, SMEM, HBM, VMEM, VMEM] + [HBM for _ in begun],
        out_specs=(VMEM, HBM),
        input_output_aliases={5: 1} if begun else {},
        scratch_shapes=[
            pltpu.VMEM((half,) + arrived.shape[1:], arrived.dtype),
            pltpu.SemaphoreType.DMA,
            pltpu.SemaphoreType.DMA,
        ],
        compiler_params=pltpu.CompilerParams(vmem_limit_bytes=LIMIT),
        cost_estimate=pl.CostEstimate(
            flops=4 * rows * half * arrived.shape[1] * head,
            bytes_accessed=2 * half * arrived.shape[1] * arrived.shape[2] * 2,
            transcendentals=rows * half * arrived.shape[1],
        ),
        name=name,
    )(info, place, arrived, queries, fresh, *begun)


def project_kernel(kept_ref, partner_ref, weight_ref, own_ref, other_ref):
    steps = own_ref.shape[0]
    rows = []
    for ref in (kept_ref, partner_ref):
        value = ref[...].astype(jnp.float32)
        rows.append(
            jnp.concatenate([value[at : at + steps] for at in range(0, value.shape[0], steps)], axis=1)
        )
    both = jnp.concatenate(rows, axis=0).astype(jnp.bfloat16)
    tile = 1024
    for at in range(0, weight_ref.shape[1], tile):
        product = jnp.dot(both, weight_ref[:, at : at + tile], preferred_element_type=jnp.float32)
        own_ref[:, at : at + tile] = product[:steps]
        other_ref[:, at : at + tile] = product[steps:].astype(jnp.bfloat16)


def project(kept, partner, weight, steps):
    wide = weight.shape[1]
    return pl.pallas_call(
        project_kernel,
        out_shape=(
            jax.ShapeDtypeStruct((steps, wide), jnp.float32),
            jax.ShapeDtypeStruct((steps, wide), jnp.bfloat16),
        ),
        in_specs=[VMEM, VMEM, VMEM],
        out_specs=(VMEM, VMEM),
        compiler_params=pltpu.CompilerParams(vmem_limit_bytes=LIMIT),
        cost_estimate=pl.CostEstimate(
            flops=4 * steps * weight.size, bytes_accessed=weight.size * 2, transcendentals=0
        ),
        name="project",
    )(kept, partner, pltpu.with_memory_space_constraint(weight, pltpu.VMEM))


def on_device(old_cache, old_weight, plan_src, plan_page, lengths, queries, new_kv):
    devices = lax.axis_size("inst") * lax.axis_size("tp")
    steps = queries.shape[1]
    width = old_cache.shape[2]
    heads = new_kv.shape[2] // width
    head = width // 2
    groups = queries.shape[2] // (heads * head)
    side = lax.axis_index("tp") % 2

    wanted, place, held = make_plan(plan_src, plan_page, old_cache, devices)
    asked = lax.all_to_all(wanted, BOTH, split_axis=0, concat_axis=0, tiled=True)
    outgoing = take(held, asked)
    outgoing = outgoing.reshape((devices, 2) + old_cache.shape[1:])
    arrived = lax.all_to_all(outgoing, BOTH, split_axis=0, concat_axis=0, tiled=True)
    arrived = arrived.reshape((devices * 2,) + old_cache.shape[1:])

    rows = queries.reshape(steps, heads, groups, head).transpose(1, 2, 0, 3)
    rows = rows.reshape(heads, groups * steps, head)
    fresh = new_kv.reshape(steps, heads, width).transpose(1, 0, 2)
    length = lax.dynamic_index_in_dim(lengths[0, :, 0], side, 0, keepdims=False)
    passed, moved = attend(1 - side, length, place, arrived, rows, fresh, None, "attend_other")
    partner = flipped(passed, 1)
    kept, moved = attend(side, length, place, arrived, rows, fresh, moved, "attend_own")

    own, other = project(kept, partner, old_weight, steps)
    own = own + flipped(other, 1).astype(jnp.float32)
    bits = 2
    while bits < lax.axis_size("tp"):
        own = own + flipped(own.astype(jnp.bfloat16), bits).astype(jnp.float32)
        bits *= 2
    return own.reshape(1, steps, -1).astype(jnp.bfloat16), moved


def solution(mesh):
    placed = (
        P(BOTH, None, None),
        P("tp", None),
        P(BOTH, None),
        P(BOTH, None),
        P("inst", None, None),
        P(BOTH, None, None),
        P(BOTH, None, None),
    )
    return jax.shard_map(
        on_device,
        mesh=mesh,
        in_specs=placed,
        out_specs=(P(BOTH, None, None), P(BOTH, None, None)),
        check_vma=False,
    )
```

```python
import functools

import jax
import jax.numpy as jnp
from jax import lax
from jax.experimental import pallas as pl
from jax.experimental.pallas import tpu as pltpu
from jax.sharding import PartitionSpec as P

BOTH = ("inst", "tp")
HBM = pl.BlockSpec(memory_space=pltpu.HBM)
VMEM = pl.BlockSpec(memory_space=pltpu.VMEM)
SMEM = pl.BlockSpec(memory_space=pltpu.SMEM)
LIMIT = 24 * 1024 * 1024


def flipped(value, bits):
    size = lax.axis_size("tp")
    return lax.ppermute(value, "tp", [(i, i ^ bits) for i in range(size)])


def in_hbm(value):
    return pltpu.with_memory_space_constraint(value, pltpu.HBM)


def plan_kernel(src_hbm, page_hbm, cache_ref, wanted_ref, place_ref, held_ref, src_ref, page_ref, sems):
    copies = [
        pltpu.make_async_copy(src_hbm, src_ref, sems.at[0]),
        pltpu.make_async_copy(page_hbm, page_ref, sems.at[1]),
        pltpu.make_async_copy(cache_ref, held_ref, sems.at[2]),
    ]
    for copy in copies:
        copy.start()
    slots = src_ref.shape[1]
    sources = wanted_ref.shape[0]
    order = lax.broadcasted_iota(jnp.int32, (1, slots), 1)
    copies[0].wait()
    copies[1].wait()
    src = src_ref[...]
    coded = order * 65536 + page_ref[...]
    named = lax.broadcasted_iota(jnp.int32, (sources, slots), 0) == src
    first = jnp.min(jnp.where(named, coded, slots * 65536), axis=1, keepdims=True)
    last = jnp.max(jnp.where(named, coded, -1), axis=1, keepdims=True)
    wanted_ref[:, 0:1] = jnp.where(last >= 0, first & 65535, -1)
    wanted_ref[:, 1:2] = jnp.where(last > first, last & 65535, -1)
    rows = lax.broadcasted_iota(jnp.int32, (slots, slots), 0)
    columns = lax.broadcasted_iota(jnp.int32, (slots, slots), 1)
    src_column = jnp.max(jnp.where(rows == columns, src, 0), axis=1, keepdims=True)
    again = jnp.max(jnp.where((src_column == src) & (rows < columns), 1, 0), axis=0, keepdims=True)
    place_ref[...] = src * 2 + again
    copies[2].wait()


def make_plan(plan_src, plan_page, pages, sources):
    slots = plan_src.shape[1]
    return pl.pallas_call(
        plan_kernel,
        out_shape=(
            jax.ShapeDtypeStruct((sources, 2), jnp.int32),
            jax.ShapeDtypeStruct((1, slots), jnp.int32),
            pltpu.VMEM(pages.shape, pages.dtype),
        ),
        in_specs=[HBM, HBM, HBM],
        out_specs=(VMEM, VMEM, VMEM),
        scratch_shapes=[
            pltpu.VMEM((1, slots), jnp.int32),
            pltpu.VMEM((1, slots), jnp.int32),
            pltpu.SemaphoreType.DMA((3,)),
        ],
        compiler_params=pltpu.CompilerParams(vmem_limit_bytes=LIMIT),
        name="make_plan",
    )(in_hbm(plan_src), in_hbm(plan_page), in_hbm(pages))


def take_kernel(at_ref, from_ref, to_ref, sem):
    columns = at_ref.shape[1]

    @pl.loop(0, at_ref.shape[0], init_carry=jnp.int32(0), unroll=4)
    def started(row, count):
        for column in range(columns):
            page = at_ref[row, column]

            @pl.when(page >= 0)
            def _():
                pltpu.make_async_copy(from_ref.at[page], to_ref.at[row * columns + column], sem).start()

            count = count + (page >= 0).astype(jnp.int32)
        return count

    @pl.loop(0, started)
    def _(_):
        pltpu.make_async_copy(from_ref.at[0], to_ref.at[0], sem).wait()


def take(pages, at):
    count = at.shape[0] * at.shape[1]
    shape = (count,) + pages.shape[1:]
    return pl.pallas_call(
        take_kernel,
        out_shape=pltpu.HBM(shape, pages.dtype),
        in_specs=[SMEM, VMEM],
        out_specs=HBM,
        scratch_shapes=[pltpu.SemaphoreType.DMA],
        compiler_params=pltpu.CompilerParams(vmem_limit_bytes=LIMIT),
        cost_estimate=pl.CostEstimate(
            flops=0, bytes_accessed=count * pages.shape[1] * pages.shape[2] * 2, transcendentals=0
        ),
        name="take_outgoing",
    )(at, pages)


def hold_kernel(weight_ref, after_ref, held_ref, sem):
    copy = pltpu.make_async_copy(weight_ref, held_ref, sem)
    copy.start()
    copy.wait()


def hold(weight, after):
    return pl.pallas_call(
        hold_kernel,
        out_shape=pltpu.VMEM(weight.shape, weight.dtype),
        in_specs=[HBM, HBM],
        out_specs=VMEM,
        scratch_shapes=[pltpu.SemaphoreType.DMA],
        compiler_params=pltpu.CompilerParams(vmem_limit_bytes=LIMIT),
        cost_estimate=pl.CostEstimate(flops=0, bytes_accessed=2 * weight.size, transcendentals=0),
        name="hold_weight",
    )(in_hbm(weight), in_hbm(after))


def attention(which, length, query_ref, fresh_ref, pages_ref, ready):
    slots, page, width = pages_ref.shape
    head = width // 2
    half = slots // 2
    parts = len(ready)
    size = half // parts
    query = query_ref[which]
    fresh = fresh_ref[which]
    rows = query.shape[0]
    steps = fresh.shape[0]
    scale = head ** (-0.5)
    contract_last = (((1,), (1,)), ((), ()))
    fresh_scores = (
        lax.dot_general(query, fresh[:, :head], contract_last, preferred_element_type=jnp.float32) * scale
    )
    step_of = lax.broadcasted_iota(jnp.int32, (rows, steps), 0) % steps
    key_step = lax.broadcasted_iota(jnp.int32, (rows, steps), 1)
    fresh_scores = jnp.where(step_of >= key_step, fresh_scores, jnp.float32(-1e30))
    highest = jnp.max(fresh_scores, axis=1, keepdims=True)
    scores = []
    for part in range(parts):
        ready[part]()
        keys = pages_ref[pl.ds(which * half + part * size, size), :, :head].reshape(size * page, head)
        found = lax.dot_general(query, keys, contract_last, preferred_element_type=jnp.float32) * scale
        position = lax.broadcasted_iota(jnp.int32, found.shape, 1) + part * size * page
        found = jnp.where(position < length, found, jnp.float32(-1e30))
        highest = jnp.maximum(highest, jnp.max(found, axis=1, keepdims=True))
        scores.append(found)
    fresh_weights = jnp.exp(fresh_scores - highest)
    total = jnp.sum(fresh_weights, axis=1, keepdims=True)
    fresh_values = fresh[:, head:].astype(jnp.float32)
    mixed = jnp.zeros((rows, head), jnp.float32)
    for step in range(steps):
        mixed = mixed + fresh_weights[:, step : step + 1] * fresh_values[step : step + 1, :]
    for part in range(parts):
        weights = jnp.exp(scores[part] - highest)
        total = total + jnp.sum(weights, axis=1, keepdims=True)
        values = pages_ref[pl.ds(which * half + part * size, size), :, head:].reshape(size * page, head)
        mixed = mixed + jnp.dot(weights.astype(jnp.bfloat16), values, preferred_element_type=jnp.float32)
    return (mixed / total).astype(jnp.bfloat16)


def other_kernel(info_ref, arrived_ref, query_ref, fresh_ref, weight_ref, out_ref, pages_ref, sems):
    slots = pages_ref.shape[0]
    half = slots // 2
    parts = sems.shape[0] - 1
    size = half // parts
    which = info_ref[slots]
    length = info_ref[slots + 1]

    def gather(first, count, sem):
        @pl.loop(0, count, unroll=8)
        def _(at):
            slot = first + at
            pltpu.make_async_copy(arrived_ref.at[info_ref[slot]], pages_ref.at[slot], sem).start()

    def wait(first, count, sem):
        block = pages_ref.at[pl.ds(first, count)]
        pltpu.make_async_copy(block, block, sem).wait()

    for part in range(parts):
        gather(which * half + part * size, size, sems.at[part])
    gather((1 - which) * half, half, sems.at[parts])
    ready = [
        functools.partial(wait, which * half + part * size, size, sems.at[part]) for part in range(parts)
    ]
    out_ref[...] = attention(which, length, query_ref, fresh_ref, pages_ref, ready)
    wait((1 - which) * half, half, sems.at[parts])


def own_kernel(info_ref, pages_ref, query_ref, fresh_ref, out_ref, moved_ref, sem):
    slots = pages_ref.shape[0]
    store = pltpu.make_async_copy(pages_ref, moved_ref, sem)
    store.start()
    which = 1 - info_ref[slots]
    out_ref[...] = attention(which, info_ref[slots + 1], query_ref, fresh_ref, pages_ref, [lambda: None])
    store.wait()


def attend_cost(slots, rows, page, head):
    return pl.CostEstimate(
        flops=2 * rows * slots * page * head,
        bytes_accessed=4 * slots * page * head,
        transcendentals=rows * slots * page // 2,
    )


def attend_other(info, arrived, queries, fresh, weight):
    rows, head = queries.shape[1:]
    slots = info.shape[0] - 2
    page = arrived.shape[1]
    return pl.pallas_call(
        other_kernel,
        out_shape=(
            jax.ShapeDtypeStruct((rows, head), jnp.bfloat16),
            pltpu.VMEM((slots,) + arrived.shape[1:], arrived.dtype),
        ),
        in_specs=[SMEM, HBM, VMEM, VMEM, VMEM],
        out_specs=(VMEM, VMEM),
        scratch_shapes=[pltpu.SemaphoreType.DMA((3,))],
        compiler_params=pltpu.CompilerParams(vmem_limit_bytes=LIMIT),
        cost_estimate=attend_cost(slots, rows, page, head),
        name="attend_other",
    )(info, in_hbm(arrived), queries, fresh, weight)


def attend_own(info, pages, queries, fresh):
    rows, head = queries.shape[1:]
    return pl.pallas_call(
        own_kernel,
        out_shape=(
            jax.ShapeDtypeStruct((rows, head), jnp.bfloat16),
            pltpu.HBM(pages.shape, pages.dtype),
        ),
        in_specs=[SMEM, VMEM, VMEM, VMEM],
        out_specs=(VMEM, HBM),
        scratch_shapes=[pltpu.SemaphoreType.DMA],
        compiler_params=pltpu.CompilerParams(vmem_limit_bytes=LIMIT),
        cost_estimate=attend_cost(pages.shape[0], rows, pages.shape[1], head),
        name="attend_own",
    )(info, pages, queries, fresh)


def project_kernel(kept_ref, partner_ref, weight_ref, sum_ref, sent_ref):
    steps = sum_ref.shape[0] // 2
    rows = []
    for ref in (kept_ref, partner_ref):
        value = ref[...].astype(jnp.float32)
        rows.append(
            jnp.concatenate([value[at : at + steps] for at in range(0, value.shape[0], steps)], axis=1)
        )
    both = jnp.concatenate(rows, axis=0).astype(jnp.bfloat16)
    tile = 1024
    for at in range(0, weight_ref.shape[1], tile):
        product = jnp.dot(both, weight_ref[:, at : at + tile], preferred_element_type=jnp.float32)
        sum_ref[:, at : at + tile] = product
        turned = jnp.concatenate([product[steps:], product[:steps]], axis=0)
        sent_ref[:, at : at + tile] = turned.astype(jnp.bfloat16)


def project(kept, partner, weight, steps):
    wide = weight.shape[1]
    return pl.pallas_call(
        project_kernel,
        out_shape=(
            jax.ShapeDtypeStruct((2 * steps, wide), jnp.float32),
            jax.ShapeDtypeStruct((2 * steps, wide), jnp.bfloat16),
        ),
        in_specs=[VMEM, VMEM, VMEM],
        out_specs=(VMEM, VMEM),
        compiler_params=pltpu.CompilerParams(vmem_limit_bytes=LIMIT),
        cost_estimate=pl.CostEstimate(
            flops=4 * steps * weight.size, bytes_accessed=weight.size * 2, transcendentals=0
        ),
        name="project",
    )(kept, partner, weight)


def on_device(old_cache, old_weight, plan_src, plan_page, lengths, queries, new_kv):
    devices = lax.axis_size("inst") * lax.axis_size("tp")
    steps = queries.shape[1]
    width = old_cache.shape[2]
    heads = new_kv.shape[2] // width
    head = width // 2
    groups = queries.shape[2] // (heads * head)
    side = lax.axis_index("tp") % 2

    wanted, place, held = make_plan(plan_src, plan_page, old_cache, devices)
    asked = lax.all_to_all(wanted, BOTH, split_axis=0, concat_axis=0, tiled=True)
    taken = take(held, asked)
    outgoing = taken.reshape((devices, 2) + old_cache.shape[1:])
    arrived = lax.all_to_all(outgoing, BOTH, split_axis=0, concat_axis=0, tiled=True)
    arrived = arrived.reshape((devices * 2,) + old_cache.shape[1:])
    weight = hold(old_weight, taken)

    rows = queries.reshape(steps, heads, groups, head).transpose(1, 2, 0, 3)
    rows = rows.reshape(heads, groups * steps, head)
    fresh = new_kv.reshape(steps, heads, width).transpose(1, 0, 2)
    length = lax.dynamic_index_in_dim(lengths[0, :, 0], side, 0, keepdims=False)
    info = jnp.concatenate([place[0], jnp.stack([1 - side, length]).astype(jnp.int32)])
    passed, pages = attend_other(info, arrived, rows, fresh, weight)
    partner = flipped(passed, 1)
    kept, moved = attend_own(info, pages, rows, fresh)

    total, sent = project(kept, partner, weight, steps)
    total = total + flipped(sent, 1).astype(jnp.float32)
    own = total[:steps] + flipped(total[steps:].astype(jnp.bfloat16), 3).astype(jnp.float32)
    bits = 4
    while bits < lax.axis_size("tp"):
        own = own + flipped(own.astype(jnp.bfloat16), bits).astype(jnp.float32)
        bits *= 2
    return own.reshape(1, steps, -1).astype(jnp.bfloat16), moved


def solution(mesh):
    placed = (
        P(BOTH, None, None),
        P("tp", None),
        P(BOTH, None),
        P(BOTH, None),
        P("inst", None, None),
        P(BOTH, None, None),
        P(BOTH, None, None),
    )
    return jax.shard_map(
        on_device,
        mesh=mesh,
        in_specs=placed,
        out_specs=(P(BOTH, None, None), P(BOTH, None, None)),
        check_vma=False,
    )
```

```python
import functools

import jax
import jax.numpy as jnp
from jax import lax
from jax.experimental import pallas as pl
from jax.experimental.pallas import tpu as pltpu
from jax.sharding import PartitionSpec as P

BOTH = ("inst", "tp")
HBM = pl.BlockSpec(memory_space=pltpu.HBM)
VMEM = pl.BlockSpec(memory_space=pltpu.VMEM)
SMEM = pl.BlockSpec(memory_space=pltpu.SMEM)
LIMIT = 6 * 1024 * 1024


def flipped(value, bits):
    size = lax.axis_size("tp")
    return lax.ppermute(value, "tp", [(i, i ^ bits) for i in range(size)])


def in_hbm(value):
    return pltpu.with_memory_space_constraint(value, pltpu.HBM)


def in_vmem(value):
    return pltpu.with_memory_space_constraint(value, pltpu.VMEM)


def plan_kernel(src_hbm, page_hbm, cache_ref, wanted_ref, place_ref, held_ref, src_ref, page_ref, sems):
    copies = [
        pltpu.make_async_copy(src_hbm, src_ref, sems.at[0]),
        pltpu.make_async_copy(page_hbm, page_ref, sems.at[1]),
        pltpu.make_async_copy(cache_ref, held_ref, sems.at[2]),
    ]
    for copy in copies:
        copy.start()
    slots = src_ref.shape[1]
    sources = wanted_ref.shape[0]
    order = lax.broadcasted_iota(jnp.int32, (1, slots), 1)
    copies[0].wait()
    copies[1].wait()
    src = src_ref[...]
    coded = order * 65536 + page_ref[...]
    named = lax.broadcasted_iota(jnp.int32, (sources, slots), 0) == src
    first = jnp.min(jnp.where(named, coded, slots * 65536), axis=1, keepdims=True)
    last = jnp.max(jnp.where(named, coded, -1), axis=1, keepdims=True)
    wanted_ref[:, 0:1] = jnp.where(last >= 0, first & 65535, -1)
    wanted_ref[:, 1:2] = jnp.where(last > first, last & 65535, -1)
    rows = lax.broadcasted_iota(jnp.int32, (slots, slots), 0)
    columns = lax.broadcasted_iota(jnp.int32, (slots, slots), 1)
    src_column = jnp.max(jnp.where(rows == columns, src, 0), axis=1, keepdims=True)
    again = jnp.max(jnp.where((src_column == src) & (rows < columns), 1, 0), axis=0, keepdims=True)
    place_ref[...] = src * 2 + again
    copies[2].wait()


def make_plan(plan_src, plan_page, pages, sources):
    slots = plan_src.shape[1]
    return pl.pallas_call(
        plan_kernel,
        out_shape=(
            jax.ShapeDtypeStruct((sources, 2), jnp.int32),
            jax.ShapeDtypeStruct((1, slots), jnp.int32),
            pltpu.VMEM(pages.shape, pages.dtype),
        ),
        in_specs=[HBM, HBM, HBM],
        out_specs=(VMEM, VMEM, VMEM),
        scratch_shapes=[
            pltpu.VMEM((1, slots), jnp.int32),
            pltpu.VMEM((1, slots), jnp.int32),
            pltpu.SemaphoreType.DMA((3,)),
        ],
        compiler_params=pltpu.CompilerParams(vmem_limit_bytes=LIMIT),
        name="make_plan",
    )(in_hbm(plan_src), in_hbm(plan_page), in_hbm(pages))


def take_kernel(at_ref, from_ref, to_ref, sem):
    columns = at_ref.shape[1]

    @pl.loop(0, at_ref.shape[0], init_carry=jnp.int32(0), unroll=4)
    def started(row, count):
        for column in range(columns):
            page = at_ref[row, column]

            @pl.when(page >= 0)
            def _():
                pltpu.make_async_copy(from_ref.at[page], to_ref.at[row * columns + column], sem).start()

            count = count + (page >= 0).astype(jnp.int32)
        return count

    @pl.loop(0, started)
    def _(_):
        pltpu.make_async_copy(from_ref.at[0], to_ref.at[0], sem).wait()


def take(pages, at):
    count = at.shape[0] * at.shape[1]
    shape = (count,) + pages.shape[1:]
    return pl.pallas_call(
        take_kernel,
        out_shape=pltpu.HBM(shape, pages.dtype),
        in_specs=[SMEM, VMEM],
        out_specs=HBM,
        scratch_shapes=[pltpu.SemaphoreType.DMA],
        compiler_params=pltpu.CompilerParams(vmem_limit_bytes=LIMIT),
        cost_estimate=pl.CostEstimate(
            flops=0, bytes_accessed=count * pages.shape[1] * pages.shape[2] * 2, transcendentals=0
        ),
        name="take_outgoing",
    )(at, in_vmem(pages))


def attention(which, length, query_ref, fresh_ref, pages_ref, ready):
    slots, page, width = pages_ref.shape
    head = width // 2
    half = slots // 2
    parts = len(ready)
    size = half // parts
    query = query_ref[which]
    fresh = fresh_ref[which]
    rows = query.shape[0]
    steps = fresh.shape[0]
    scale = head ** (-0.5)
    contract_last = (((1,), (1,)), ((), ()))
    fresh_scores = (
        lax.dot_general(query, fresh[:, :head], contract_last, preferred_element_type=jnp.float32) * scale
    )
    step_of = lax.broadcasted_iota(jnp.int32, (rows, steps), 0) % steps
    key_step = lax.broadcasted_iota(jnp.int32, (rows, steps), 1)
    fresh_scores = jnp.where(step_of >= key_step, fresh_scores, jnp.float32(-1e30))
    highest = jnp.max(fresh_scores, axis=1, keepdims=True)
    scores = []
    for part in range(parts):
        ready[part]()
        keys = pages_ref[pl.ds(which * half + part * size, size), :, :head].reshape(size * page, head)
        found = lax.dot_general(query, keys, contract_last, preferred_element_type=jnp.float32) * scale
        position = lax.broadcasted_iota(jnp.int32, found.shape, 1) + part * size * page
        found = jnp.where(position < length, found, jnp.float32(-1e30))
        highest = jnp.maximum(highest, jnp.max(found, axis=1, keepdims=True))
        scores.append(found)
    fresh_weights = jnp.exp(fresh_scores - highest)
    total = jnp.sum(fresh_weights, axis=1, keepdims=True)
    fresh_values = fresh[:, head:].astype(jnp.float32)
    mixed = jnp.zeros((rows, head), jnp.float32)
    for step in range(steps):
        mixed = mixed + fresh_weights[:, step : step + 1] * fresh_values[step : step + 1, :]
    for part in range(parts):
        weights = jnp.exp(scores[part] - highest)
        total = total + jnp.sum(weights, axis=1, keepdims=True)
        values = pages_ref[pl.ds(which * half + part * size, size), :, head:].reshape(size * page, head)
        mixed = mixed + jnp.dot(weights.astype(jnp.bfloat16), values, preferred_element_type=jnp.float32)
    return (mixed / total).astype(jnp.bfloat16)


def other_kernel(info_ref, arrived_ref, query_ref, fresh_ref, weight_ref, *rest):
    out_ref, pages_ref, held_ref, sems, held_sem = rest
    slots = pages_ref.shape[0]
    half = slots // 2
    parts = sems.shape[0] - 1
    size = half // parts
    which = info_ref[slots]
    length = info_ref[slots + 1]

    def gather(first, count, sem):
        @pl.loop(0, count, unroll=8)
        def _(at):
            slot = first + at
            pltpu.make_async_copy(arrived_ref.at[info_ref[slot]], pages_ref.at[slot], sem).start()

    def wait(first, count, sem):
        block = pages_ref.at[pl.ds(first, count)]
        pltpu.make_async_copy(block, block, sem).wait()

    for part in range(parts):
        gather(which * half + part * size, size, sems.at[part])
    gather((1 - which) * half, half, sems.at[parts])
    hold = pltpu.make_async_copy(weight_ref.at[pl.ds(0, held_ref.shape[0])], held_ref, held_sem)
    hold.start()
    ready = [
        functools.partial(wait, which * half + part * size, size, sems.at[part]) for part in range(parts)
    ]
    out_ref[...] = attention(which, length, query_ref, fresh_ref, pages_ref, ready)
    wait((1 - which) * half, half, sems.at[parts])
    hold.wait()


def own_kernel(info_ref, pages_ref, query_ref, fresh_ref, weight_ref, *rest):
    out_ref, held_ref, held_sem = rest
    slots = pages_ref.shape[0]
    count = held_ref.shape[0]
    hold = pltpu.make_async_copy(
        weight_ref.at[pl.ds(weight_ref.shape[0] - count, count)], held_ref, held_sem
    )
    hold.start()
    which = 1 - info_ref[slots]
    out_ref[...] = attention(which, info_ref[slots + 1], query_ref, fresh_ref, pages_ref, [lambda: None])
    hold.wait()


def attend_cost(slots, rows, page, head):
    return pl.CostEstimate(
        flops=2 * rows * slots * page * head,
        bytes_accessed=4 * slots * page * head,
        transcendentals=rows * slots * page // 2,
    )


def attend_other(info, arrived, queries, fresh, weight, count):
    rows, head = queries.shape[1:]
    slots = info.shape[0] - 2
    page = arrived.shape[1]
    return pl.pallas_call(
        other_kernel,
        out_shape=(
            jax.ShapeDtypeStruct((rows, head), jnp.bfloat16),
            pltpu.VMEM((slots,) + arrived.shape[1:], arrived.dtype),
            pltpu.VMEM((count, weight.shape[1]), weight.dtype),
        ),
        in_specs=[SMEM, HBM, VMEM, VMEM, HBM],
        out_specs=(VMEM, VMEM, VMEM),
        scratch_shapes=[pltpu.SemaphoreType.DMA((3,)), pltpu.SemaphoreType.DMA],
        compiler_params=pltpu.CompilerParams(vmem_limit_bytes=LIMIT),
        cost_estimate=attend_cost(slots, rows, page, head),
        name="attend_other",
    )(info, in_hbm(arrived), queries, fresh, in_hbm(weight))


def attend_own(info, pages, queries, fresh, weight, count):
    rows, head = queries.shape[1:]
    return pl.pallas_call(
        own_kernel,
        out_shape=(
            jax.ShapeDtypeStruct((rows, head), jnp.bfloat16),
            pltpu.VMEM((count, weight.shape[1]), weight.dtype),
        ),
        in_specs=[SMEM, VMEM, VMEM, VMEM, HBM],
        out_specs=(VMEM, VMEM),
        scratch_shapes=[pltpu.SemaphoreType.DMA],
        compiler_params=pltpu.CompilerParams(vmem_limit_bytes=LIMIT),
        cost_estimate=attend_cost(pages.shape[0], rows, pages.shape[1], head),
        name="attend_own",
    )(info, in_vmem(pages), queries, fresh, in_hbm(weight))


def store_kernel(pages_ref, _, moved_ref, sem):
    copy = pltpu.make_async_copy(pages_ref, moved_ref, sem)
    copy.start()
    copy.wait()


def store(pages, after):
    return pl.pallas_call(
        store_kernel,
        out_shape=pltpu.HBM(pages.shape, pages.dtype),
        in_specs=[VMEM, VMEM],
        out_specs=HBM,
        scratch_shapes=[pltpu.SemaphoreType.DMA],
        compiler_params=pltpu.CompilerParams(vmem_limit_bytes=LIMIT),
        cost_estimate=pl.CostEstimate(flops=0, bytes_accessed=2 * pages.size, transcendentals=0),
        name="store_moved",
    )(in_vmem(pages), in_vmem(after))


def project_kernel(kept_ref, partner_ref, first_ref, second_ref, sum_ref, sent_ref):
    steps = sum_ref.shape[0] // 2
    rows = []
    for ref in (kept_ref, partner_ref):
        value = ref[...].astype(jnp.float32)
        rows.append(
            jnp.concatenate([value[at : at + steps] for at in range(0, value.shape[0], steps)], axis=1)
        )
    both = jnp.concatenate(rows, axis=0).astype(jnp.bfloat16)
    tile = 1024
    cut = first_ref.shape[0]
    for at in range(0, first_ref.shape[1], tile):
        product = jnp.dot(both[:, :cut], first_ref[:, at : at + tile], preferred_element_type=jnp.float32)
        product = product + jnp.dot(
            both[:, cut:], second_ref[:, at : at + tile], preferred_element_type=jnp.float32
        )
        sum_ref[:, at : at + tile] = product
        turned = jnp.concatenate([product[steps:], product[:steps]], axis=0)
        sent_ref[:, at : at + tile] = turned.astype(jnp.bfloat16)


def project(kept, partner, first, second, steps):
    wide = first.shape[1]
    return pl.pallas_call(
        project_kernel,
        out_shape=(
            jax.ShapeDtypeStruct((2 * steps, wide), jnp.float32),
            jax.ShapeDtypeStruct((2 * steps, wide), jnp.bfloat16),
        ),
        in_specs=[VMEM, VMEM, VMEM, VMEM],
        out_specs=(VMEM, VMEM),
        compiler_params=pltpu.CompilerParams(vmem_limit_bytes=LIMIT),
        cost_estimate=pl.CostEstimate(
            flops=4 * steps * (first.size + second.size),
            bytes_accessed=2 * (first.size + second.size),
            transcendentals=0,
        ),
        name="project",
    )(kept, partner, in_vmem(first), in_vmem(second))


def on_device(old_cache, old_weight, plan_src, plan_page, lengths, queries, new_kv):
    devices = lax.axis_size("inst") * lax.axis_size("tp")
    steps = queries.shape[1]
    width = old_cache.shape[2]
    heads = new_kv.shape[2] // width
    head = width // 2
    groups = queries.shape[2] // (heads * head)
    side = lax.axis_index("tp") % 2

    wanted, place, held = make_plan(plan_src, plan_page, old_cache, devices)
    asked = lax.all_to_all(wanted, BOTH, split_axis=0, concat_axis=0, tiled=True)
    taken = take(held, asked)
    outgoing = taken.reshape((devices, 2) + old_cache.shape[1:])
    arrived = lax.all_to_all(outgoing, BOTH, split_axis=0, concat_axis=0, tiled=True)
    arrived = arrived.reshape((devices * 2,) + old_cache.shape[1:])

    rows = queries.reshape(steps, heads, groups, head).transpose(1, 2, 0, 3)
    rows = rows.reshape(heads, groups * steps, head)
    fresh = new_kv.reshape(steps, heads, width).transpose(1, 0, 2)
    length = lax.dynamic_index_in_dim(lengths[0, :, 0], side, 0, keepdims=False)
    info = jnp.concatenate([place[0], jnp.stack([1 - side, length]).astype(jnp.int32)])
    early = old_weight.shape[0] // 4
    passed, pages, first = attend_other(info, arrived, rows, fresh, old_weight, early)
    partner = flipped(passed, 1)
    kept, second = attend_own(info, pages, rows, fresh, old_weight, old_weight.shape[0] - early)

    total, sent = project(kept, partner, first, second, steps)
    moved = store(pages, sent)
    total = total + flipped(sent, 1).astype(jnp.float32)
    rounded = total.astype(jnp.bfloat16)
    own = total[:steps]
    for high in range(0, lax.axis_size("tp"), 4):
        for low in (0, 3):
            if high + low:
                rows = rounded[:steps] if low == 0 else rounded[steps:]
                own = own + flipped(rows, high + low).astype(jnp.float32)
    return own.reshape(1, steps, -1).astype(jnp.bfloat16), moved


def solution(mesh):
    placed = (
        P(BOTH, None, None),
        P("tp", None),
        P(BOTH, None),
        P(BOTH, None),
        P("inst", None, None),
        P(BOTH, None, None),
        P(BOTH, None, None),
    )
    return jax.shard_map(
        on_device,
        mesh=mesh,
        in_specs=placed,
        out_specs=(P(BOTH, None, None), P(BOTH, None, None)),
        check_vma=False,
    )
```

```python
import functools

import jax
import jax.numpy as jnp
from jax import lax
from jax.experimental import pallas as pl
from jax.experimental.pallas import tpu as pltpu
from jax.sharding import PartitionSpec as P

BOTH = ("inst", "tp")
HBM = pl.BlockSpec(memory_space=pltpu.HBM)
VMEM = pl.BlockSpec(memory_space=pltpu.VMEM)
SMEM = pl.BlockSpec(memory_space=pltpu.SMEM)
LIMIT = 6 * 1024 * 1024


def flipped(value, bits):
    size = lax.axis_size("tp")
    return lax.ppermute(value, "tp", [(i, i ^ bits) for i in range(size)])


def in_hbm(value):
    return pltpu.with_memory_space_constraint(value, pltpu.HBM)


def in_vmem(value):
    return pltpu.with_memory_space_constraint(value, pltpu.VMEM)


def plan_kernel(src_hbm, page_hbm, cache_ref, wanted_ref, place_ref, held_ref, src_ref, page_ref, sems):
    copies = [
        pltpu.make_async_copy(src_hbm, src_ref, sems.at[0]),
        pltpu.make_async_copy(page_hbm, page_ref, sems.at[1]),
        pltpu.make_async_copy(cache_ref, held_ref, sems.at[2]),
    ]
    for copy in copies:
        copy.start()
    slots = src_ref.shape[1]
    sources = wanted_ref.shape[0]
    order = lax.broadcasted_iota(jnp.int32, (1, slots), 1)
    copies[0].wait()
    copies[1].wait()
    src = src_ref[...]
    coded = order * 65536 + page_ref[...]
    named = lax.broadcasted_iota(jnp.int32, (sources, slots), 0) == src
    first = jnp.min(jnp.where(named, coded, slots * 65536), axis=1, keepdims=True)
    last = jnp.max(jnp.where(named, coded, -1), axis=1, keepdims=True)
    wanted_ref[:, 0:1] = jnp.where(last >= 0, first & 65535, -1)
    wanted_ref[:, 1:2] = jnp.where(last > first, last & 65535, -1)
    rows = lax.broadcasted_iota(jnp.int32, (slots, slots), 0)
    columns = lax.broadcasted_iota(jnp.int32, (slots, slots), 1)
    src_column = jnp.max(jnp.where(rows == columns, src, 0), axis=1, keepdims=True)
    again = jnp.max(jnp.where((src_column == src) & (rows < columns), 1, 0), axis=0, keepdims=True)
    place_ref[...] = src * 2 + again
    copies[2].wait()


def make_plan(plan_src, plan_page, pages, sources):
    slots = plan_src.shape[1]
    return pl.pallas_call(
        plan_kernel,
        out_shape=(
            jax.ShapeDtypeStruct((sources, 2), jnp.int32),
            jax.ShapeDtypeStruct((1, slots), jnp.int32),
            pltpu.VMEM(pages.shape, pages.dtype),
        ),
        in_specs=[HBM, HBM, HBM],
        out_specs=(VMEM, VMEM, VMEM),
        scratch_shapes=[
            pltpu.VMEM((1, slots), jnp.int32),
            pltpu.VMEM((1, slots), jnp.int32),
            pltpu.SemaphoreType.DMA((3,)),
        ],
        compiler_params=pltpu.CompilerParams(vmem_limit_bytes=LIMIT),
        name="make_plan",
    )(in_hbm(plan_src), in_hbm(plan_page), in_hbm(pages))


def take_kernel(asked_ref, from_ref, to_ref, turned_ref, at_ref, sem, at_sem):
    count, columns = asked_ref.shape
    same = lax.broadcasted_iota(jnp.int32, (count, count), 0) == lax.broadcasted_iota(
        jnp.int32, (count, count), 1
    )
    for column in range(columns):
        turned_ref[column : column + 1, :] = jnp.sum(
            jnp.where(same, asked_ref[:, column : column + 1], 0), axis=0, keepdims=True
        )
    scalars = pltpu.make_async_copy(turned_ref, at_ref, at_sem)
    scalars.start()
    scalars.wait()

    @pl.loop(0, count, init_carry=jnp.int32(0), unroll=4)
    def started(row, count):
        for column in range(columns):
            page = at_ref[column, row]

            @pl.when(page >= 0)
            def _():
                pltpu.make_async_copy(from_ref.at[page], to_ref.at[row * columns + column], sem).start()

            count = count + (page >= 0).astype(jnp.int32)
        return count

    @pl.loop(0, started)
    def _(_):
        pltpu.make_async_copy(from_ref.at[0], to_ref.at[0], sem).wait()


def take(pages, at):
    count = at.shape[0] * at.shape[1]
    shape = (count,) + pages.shape[1:]
    return pl.pallas_call(
        take_kernel,
        out_shape=pltpu.HBM(shape, pages.dtype),
        in_specs=[VMEM, VMEM],
        out_specs=HBM,
        scratch_shapes=[
            pltpu.VMEM(at.shape[::-1], jnp.int32),
            pltpu.SMEM(at.shape[::-1], jnp.int32),
            pltpu.SemaphoreType.DMA,
            pltpu.SemaphoreType.DMA,
        ],
        compiler_params=pltpu.CompilerParams(vmem_limit_bytes=LIMIT),
        cost_estimate=pl.CostEstimate(
            flops=0, bytes_accessed=count * pages.shape[1] * pages.shape[2] * 2, transcendentals=0
        ),
        name="take_outgoing",
    )(at, in_vmem(pages))


def attention(which, length, query_ref, fresh_ref, pages_ref, ready):
    slots, page, width = pages_ref.shape
    head = width // 2
    half = slots // 2
    parts = len(ready)
    size = half // parts
    query = query_ref[which]
    fresh = fresh_ref[which]
    rows = query.shape[0]
    steps = fresh.shape[0]
    scale = head ** (-0.5)
    contract_last = (((1,), (1,)), ((), ()))
    fresh_scores = (
        lax.dot_general(query, fresh[:, :head], contract_last, preferred_element_type=jnp.float32) * scale
    )
    step_of = lax.broadcasted_iota(jnp.int32, (rows, steps), 0) % steps
    key_step = lax.broadcasted_iota(jnp.int32, (rows, steps), 1)
    fresh_scores = jnp.where(step_of >= key_step, fresh_scores, jnp.float32(-1e30))
    highest = jnp.max(fresh_scores, axis=1, keepdims=True)
    scores = []
    for part in range(parts):
        ready[part]()
        keys = pages_ref[pl.ds(which * half + part * size, size), :, :head].reshape(size * page, head)
        found = lax.dot_general(query, keys, contract_last, preferred_element_type=jnp.float32) * scale
        position = lax.broadcasted_iota(jnp.int32, found.shape, 1) + part * size * page
        found = jnp.where(position < length, found, jnp.float32(-1e30))
        highest = jnp.maximum(highest, jnp.max(found, axis=1, keepdims=True))
        scores.append(found)
    fresh_weights = jnp.exp(fresh_scores - highest)
    total = jnp.sum(fresh_weights, axis=1, keepdims=True)
    fresh_values = fresh[:, head:].astype(jnp.float32)
    mixed = jnp.zeros((rows, head), jnp.float32)
    for step in range(steps):
        mixed = mixed + fresh_weights[:, step : step + 1] * fresh_values[step : step + 1, :]
    for part in range(parts):
        weights = jnp.exp(scores[part] - highest)
        total = total + jnp.sum(weights, axis=1, keepdims=True)
        values = pages_ref[pl.ds(which * half + part * size, size), :, head:].reshape(size * page, head)
        mixed = mixed + jnp.dot(weights.astype(jnp.bfloat16), values, preferred_element_type=jnp.float32)
    return (mixed / total).astype(jnp.bfloat16)


def other_kernel(info_ref, arrived_ref, query_ref, fresh_ref, weight_ref, *rest):
    out_ref, pages_ref, held_ref, sems, held_sem = rest
    slots = pages_ref.shape[0]
    half = slots // 2
    parts = sems.shape[0] - 1
    size = half // parts
    which = info_ref[slots]
    length = info_ref[slots + 1]

    def gather(first, count, sem):
        @pl.loop(0, count, unroll=8)
        def _(at):
            slot = first + at
            pltpu.make_async_copy(arrived_ref.at[info_ref[slot]], pages_ref.at[slot], sem).start()

    def wait(first, count, sem):
        block = pages_ref.at[pl.ds(first, count)]
        pltpu.make_async_copy(block, block, sem).wait()

    for part in range(parts):
        gather(which * half + part * size, size, sems.at[part])
    gather((1 - which) * half, half, sems.at[parts])
    hold = pltpu.make_async_copy(weight_ref.at[pl.ds(0, held_ref.shape[0])], held_ref, held_sem)
    hold.start()
    ready = [
        functools.partial(wait, which * half + part * size, size, sems.at[part]) for part in range(parts)
    ]
    out_ref[...] = attention(which, length, query_ref, fresh_ref, pages_ref, ready)
    wait((1 - which) * half, half, sems.at[parts])
    hold.wait()


def own_kernel(info_ref, pages_ref, query_ref, fresh_ref, weight_ref, *rest):
    out_ref, held_ref, held_sem = rest
    slots = pages_ref.shape[0]
    count = held_ref.shape[0]
    hold = pltpu.make_async_copy(
        weight_ref.at[pl.ds(weight_ref.shape[0] - count, count)], held_ref, held_sem
    )
    hold.start()
    which = 1 - info_ref[slots]
    out_ref[...] = attention(which, info_ref[slots + 1], query_ref, fresh_ref, pages_ref, [lambda: None])
    hold.wait()


def attend_cost(slots, rows, page, head):
    return pl.CostEstimate(
        flops=2 * rows * slots * page * head,
        bytes_accessed=4 * slots * page * head,
        transcendentals=rows * slots * page // 2,
    )


def attend_other(info, arrived, queries, fresh, weight, count):
    rows, head = queries.shape[1:]
    slots = info.shape[0] - 2
    page = arrived.shape[1]
    return pl.pallas_call(
        other_kernel,
        out_shape=(
            jax.ShapeDtypeStruct((rows, head), jnp.bfloat16),
            pltpu.VMEM((slots,) + arrived.shape[1:], arrived.dtype),
            pltpu.VMEM((count, weight.shape[1]), weight.dtype),
        ),
        in_specs=[SMEM, HBM, VMEM, VMEM, HBM],
        out_specs=(VMEM, VMEM, VMEM),
        scratch_shapes=[pltpu.SemaphoreType.DMA((3,)), pltpu.SemaphoreType.DMA],
        compiler_params=pltpu.CompilerParams(vmem_limit_bytes=LIMIT),
        cost_estimate=attend_cost(slots, rows, page, head),
        name="attend_other",
    )(info, in_hbm(arrived), queries, fresh, in_hbm(weight))


def attend_own(info, pages, queries, fresh, weight, count):
    rows, head = queries.shape[1:]
    return pl.pallas_call(
        own_kernel,
        out_shape=(
            jax.ShapeDtypeStruct((rows, head), jnp.bfloat16),
            pltpu.VMEM((count, weight.shape[1]), weight.dtype),
        ),
        in_specs=[SMEM, VMEM, VMEM, VMEM, HBM],
        out_specs=(VMEM, VMEM),
        scratch_shapes=[pltpu.SemaphoreType.DMA],
        compiler_params=pltpu.CompilerParams(vmem_limit_bytes=LIMIT),
        cost_estimate=attend_cost(pages.shape[0], rows, pages.shape[1], head),
        name="attend_own",
    )(info, in_vmem(pages), queries, fresh, in_hbm(weight))


def store_kernel(pages_ref, _, moved_ref, sem):
    copy = pltpu.make_async_copy(pages_ref, moved_ref, sem)
    copy.start()
    copy.wait()


def store(pages, after):
    return pl.pallas_call(
        store_kernel,
        out_shape=pltpu.HBM(pages.shape, pages.dtype),
        in_specs=[VMEM, VMEM],
        out_specs=HBM,
        scratch_shapes=[pltpu.SemaphoreType.DMA],
        compiler_params=pltpu.CompilerParams(vmem_limit_bytes=LIMIT),
        cost_estimate=pl.CostEstimate(flops=0, bytes_accessed=2 * pages.size, transcendentals=0),
        name="store_moved",
    )(in_vmem(pages), in_vmem(after))


def project_kernel(kept_ref, partner_ref, first_ref, second_ref, sum_ref, sent_ref):
    steps = sum_ref.shape[0] // 2
    rows = []
    for ref in (kept_ref, partner_ref):
        value = ref[...].astype(jnp.float32)
        rows.append(
            jnp.concatenate([value[at : at + steps] for at in range(0, value.shape[0], steps)], axis=1)
        )
    both = jnp.concatenate(rows, axis=0).astype(jnp.bfloat16)
    tile = 1024
    cut = first_ref.shape[0]
    for at in range(0, first_ref.shape[1], tile):
        product = jnp.dot(both[:, :cut], first_ref[:, at : at + tile], preferred_element_type=jnp.float32)
        product = product + jnp.dot(
            both[:, cut:], second_ref[:, at : at + tile], preferred_element_type=jnp.float32
        )
        sum_ref[:, at : at + tile] = product
        turned = jnp.concatenate([product[steps:], product[:steps]], axis=0)
        sent_ref[:, at : at + tile] = turned.astype(jnp.bfloat16)


def project(kept, partner, first, second, steps):
    wide = first.shape[1]
    return pl.pallas_call(
        project_kernel,
        out_shape=(
            jax.ShapeDtypeStruct((2 * steps, wide), jnp.float32),
            jax.ShapeDtypeStruct((2 * steps, wide), jnp.bfloat16),
        ),
        in_specs=[VMEM, VMEM, VMEM, VMEM],
        out_specs=(VMEM, VMEM),
        compiler_params=pltpu.CompilerParams(vmem_limit_bytes=LIMIT),
        cost_estimate=pl.CostEstimate(
            flops=4 * steps * (first.size + second.size),
            bytes_accessed=2 * (first.size + second.size),
            transcendentals=0,
        ),
        name="project",
    )(kept, partner, in_vmem(first), in_vmem(second))


def on_device(old_cache, old_weight, plan_src, plan_page, lengths, queries, new_kv):
    devices = lax.axis_size("inst") * lax.axis_size("tp")
    steps = queries.shape[1]
    width = old_cache.shape[2]
    heads = new_kv.shape[2] // width
    head = width // 2
    groups = queries.shape[2] // (heads * head)
    side = lax.axis_index("tp") % 2

    wanted, place, held = make_plan(plan_src, plan_page, old_cache, devices)
    asked = lax.all_to_all(wanted, BOTH, split_axis=0, concat_axis=0, tiled=True)
    taken = take(held, asked)
    outgoing = taken.reshape((devices, 2) + old_cache.shape[1:])
    arrived = lax.all_to_all(outgoing, BOTH, split_axis=0, concat_axis=0, tiled=True)
    arrived = arrived.reshape((devices * 2,) + old_cache.shape[1:])

    rows = queries.reshape(steps, heads, groups, head).transpose(1, 2, 0, 3)
    rows = rows.reshape(heads, groups * steps, head)
    fresh = new_kv.reshape(steps, heads, width).transpose(1, 0, 2)
    length = lax.dynamic_index_in_dim(lengths[0, :, 0], side, 0, keepdims=False)
    info = jnp.concatenate([place[0], jnp.stack([1 - side, length]).astype(jnp.int32)])
    early = old_weight.shape[0] // 4
    passed, pages, first = attend_other(info, arrived, rows, fresh, old_weight, early)
    partner = flipped(passed, 1)
    kept, second = attend_own(info, pages, rows, fresh, old_weight, old_weight.shape[0] - early)

    total, sent = project(kept, partner, first, second, steps)
    moved = store(pages, sent)
    mine = sent[steps:]
    theirs = sent[:steps]
    own = total[:steps]
    own = own + flipped(theirs, 1).astype(jnp.float32) + flipped(theirs, 3).astype(jnp.float32)
    own = own + flipped(mine, 2).astype(jnp.float32)
    own = own + flipped(own.astype(jnp.bfloat16), 4).astype(jnp.float32)
    return own.reshape(1, steps, -1).astype(jnp.bfloat16), moved


def solution(mesh):
    placed = (
        P(BOTH, None, None),
        P("tp", None),
        P(BOTH, None),
        P(BOTH, None),
        P("inst", None, None),
        P(BOTH, None, None),
        P(BOTH, None, None),
    )
    return jax.shard_map(
        on_device,
        mesh=mesh,
        in_specs=placed,
        out_specs=(P(BOTH, None, None), P(BOTH, None, None)),
        check_vma=False,
    )
```

```python
import functools

import jax
import jax.numpy as jnp
from jax import lax
from jax.experimental import pallas as pl
from jax.experimental.pallas import tpu as pltpu
from jax.sharding import PartitionSpec as P

BOTH = ("inst", "tp")
HBM = pl.BlockSpec(memory_space=pltpu.HBM)
VMEM = pl.BlockSpec(memory_space=pltpu.VMEM)
SMEM = pl.BlockSpec(memory_space=pltpu.SMEM)
LIMIT = 6 * 1024 * 1024


def flipped(value, bits):
    size = lax.axis_size("tp")
    return lax.ppermute(value, "tp", [(i, i ^ bits) for i in range(size)])


def in_hbm(value):
    return pltpu.with_memory_space_constraint(value, pltpu.HBM)


def in_vmem(value):
    return pltpu.with_memory_space_constraint(value, pltpu.VMEM)


def plan_kernel(tensor, src_hbm, page_hbm, length_hbm, cache_ref, *rest):
    wanted_ref, place_ref, held_ref, src_ref, page_ref, length_ref, sems = rest
    copies = [
        pltpu.make_async_copy(src_hbm, src_ref, sems.at[0]),
        pltpu.make_async_copy(page_hbm, page_ref, sems.at[1]),
        pltpu.make_async_copy(cache_ref, held_ref, sems.at[2]),
        pltpu.make_async_copy(length_hbm, length_ref, sems.at[3]),
    ]
    for copy in copies:
        copy.start()
    slots = src_ref.shape[1]
    pairs, most = wanted_ref.shape
    side = lax.axis_index("inst") % 2
    shift = tensor.bit_length() - 1
    rows = lax.broadcasted_iota(jnp.int32, (slots, slots), 0)
    columns = lax.broadcasted_iota(jnp.int32, (slots, slots), 1)
    copies[0].wait()
    copies[1].wait()
    src = src_ref[...]
    row_of = lax.shift_right_logical(src, shift)
    pair = lax.shift_left(lax.shift_right_logical(row_of, 1), shift) + (src & (tensor - 1))
    value = page_ref[...] + jnp.where((row_of & 1) == side, 0, cache_ref.shape[0])
    pair_column = jnp.max(jnp.where(rows == columns, pair, 0), axis=1, keepdims=True)
    rank = jnp.sum(jnp.where((pair_column == pair) & (rows < columns), 1, 0), axis=0, keepdims=True)
    named = lax.broadcasted_iota(jnp.int32, (pairs, slots), 0) == pair
    for at in range(most):
        wanted_ref[:, at : at + 1] = jnp.max(
            jnp.where(named & (rank == at), value, -1), axis=1, keepdims=True
        )
    place_ref[:, :slots] = pair * most + rank
    copies[3].wait()
    group = lax.axis_index("tp") % 2
    length = jnp.where(group == 0, length_ref[0, 0], length_ref[0, 1])
    lanes = lax.broadcasted_iota(jnp.int32, (1, place_ref.shape[1] - slots), 1)
    place_ref[:, slots:] = jnp.where(lanes == 0, 1 - group, length)
    copies[2].wait()


def make_plan(plan_src, plan_page, lengths, pages, pairs, tensor):
    slots = plan_src.shape[1]
    return pl.pallas_call(
        functools.partial(plan_kernel, tensor),
        out_shape=(
            jax.ShapeDtypeStruct((pairs, 4), jnp.int32),
            jax.ShapeDtypeStruct((1, slots + 128), jnp.int32),
            pltpu.VMEM(pages.shape, pages.dtype),
        ),
        in_specs=[HBM, HBM, HBM, HBM],
        out_specs=(VMEM, VMEM, VMEM),
        scratch_shapes=[
            pltpu.VMEM((1, slots), jnp.int32),
            pltpu.VMEM((1, slots), jnp.int32),
            pltpu.SMEM(lengths.shape, jnp.int32),
            pltpu.SemaphoreType.DMA((4,)),
        ],
        compiler_params=pltpu.CompilerParams(vmem_limit_bytes=LIMIT),
        name="make_plan",
    )(in_hbm(plan_src), in_hbm(plan_page), in_hbm(lengths), in_hbm(pages))


def take_kernel(asked_ref, own_ref, other_ref, to_ref, turned_ref, at_ref, sem, at_sem):
    count, columns = asked_ref.shape
    pages = own_ref.shape[0]
    shape = (count, turned_ref.shape[1])
    same = lax.broadcasted_iota(jnp.int32, shape, 0) == lax.broadcasted_iota(jnp.int32, shape, 1)
    for column in range(columns):
        turned_ref[column : column + 1, :] = jnp.sum(
            jnp.where(same, asked_ref[:, column : column + 1], 0), axis=0, keepdims=True
        )
    scalars = pltpu.make_async_copy(turned_ref, at_ref, at_sem)
    scalars.start()
    scalars.wait()

    @pl.loop(0, count, init_carry=jnp.int32(0), unroll=2)
    def started(row, total):
        for column in range(columns):
            page = at_ref[column, row]
            to = to_ref.at[row * columns + column]

            @pl.when((page >= 0) & (page < pages))
            def _():
                pltpu.make_async_copy(own_ref.at[page], to, sem).start()

            @pl.when(page >= pages)
            def _():
                pltpu.make_async_copy(other_ref.at[page - pages], to, sem).start()

            total = total + (page >= 0).astype(jnp.int32)
        return total

    @pl.loop(0, started)
    def _(_):
        pltpu.make_async_copy(own_ref.at[0], to_ref.at[0], sem).wait()


def take(own, other, at):
    count = at.shape[0] * at.shape[1]
    shape = (count,) + own.shape[1:]
    turned = (at.shape[1], -(-at.shape[0] // 128) * 128)
    return pl.pallas_call(
        take_kernel,
        out_shape=pltpu.HBM(shape, own.dtype),
        in_specs=[VMEM, VMEM, VMEM],
        out_specs=HBM,
        scratch_shapes=[
            pltpu.VMEM(turned, jnp.int32),
            pltpu.SMEM(turned, jnp.int32),
            pltpu.SemaphoreType.DMA,
            pltpu.SemaphoreType.DMA,
        ],
        compiler_params=pltpu.CompilerParams(vmem_limit_bytes=LIMIT),
        cost_estimate=pl.CostEstimate(
            flops=0, bytes_accessed=count * own.shape[1] * own.shape[2] * 2, transcendentals=0
        ),
        name="take_outgoing",
    )(at, in_vmem(own), in_vmem(other))


def attention(which, length, query_ref, fresh_ref, pages_ref, ready):
    slots, page, width = pages_ref.shape
    head = width // 2
    half = slots // 2
    parts = len(ready)
    size = half // parts
    query = query_ref[which]
    fresh = fresh_ref[which]
    rows = query.shape[0]
    steps = fresh.shape[0]
    scale = head ** (-0.5)
    contract_last = (((1,), (1,)), ((), ()))
    fresh_scores = (
        lax.dot_general(query, fresh[:, :head], contract_last, preferred_element_type=jnp.float32) * scale
    )
    step_of = lax.broadcasted_iota(jnp.int32, (rows, steps), 0) % steps
    key_step = lax.broadcasted_iota(jnp.int32, (rows, steps), 1)
    fresh_scores = jnp.where(step_of >= key_step, fresh_scores, jnp.float32(-1e30))
    highest = jnp.max(fresh_scores, axis=1, keepdims=True)
    scores = []
    for part in range(parts):
        ready[part]()
        keys = pages_ref[pl.ds(which * half + part * size, size), :, :head].reshape(size * page, head)
        found = lax.dot_general(query, keys, contract_last, preferred_element_type=jnp.float32) * scale
        position = lax.broadcasted_iota(jnp.int32, found.shape, 1) + part * size * page
        found = jnp.where(position < length, found, jnp.float32(-1e30))
        highest = jnp.maximum(highest, jnp.max(found, axis=1, keepdims=True))
        scores.append(found)
    fresh_weights = jnp.exp(fresh_scores - highest)
    total = jnp.sum(fresh_weights, axis=1, keepdims=True)
    fresh_values = fresh[:, head:].astype(jnp.float32)
    mixed = jnp.zeros((rows, head), jnp.float32)
    for step in range(steps):
        mixed = mixed + fresh_weights[:, step : step + 1] * fresh_values[step : step + 1, :]
    for part in range(parts):
        weights = jnp.exp(scores[part] - highest)
        total = total + jnp.sum(weights, axis=1, keepdims=True)
        values = pages_ref[pl.ds(which * half + part * size, size), :, head:].reshape(size * page, head)
        mixed = mixed + jnp.dot(weights.astype(jnp.bfloat16), values, preferred_element_type=jnp.float32)
    return (mixed / total).astype(jnp.bfloat16)


def other_kernel(info_ref, arrived_ref, query_ref, fresh_ref, weight_ref, *rest):
    out_ref, pages_ref, held_ref, sems, held_sem = rest
    slots = pages_ref.shape[0]
    half = slots // 2
    parts = sems.shape[0] - 1
    size = half // parts
    which = info_ref[0, slots]
    length = info_ref[0, slots + 1]

    def gather(first, count, sem):
        @pl.loop(0, count, unroll=8)
        def _(at):
            slot = first + at
            pltpu.make_async_copy(arrived_ref.at[info_ref[0, slot]], pages_ref.at[slot], sem).start()

    def wait(first, count, sem):
        block = pages_ref.at[pl.ds(first, count)]
        pltpu.make_async_copy(block, block, sem).wait()

    for part in range(parts):
        gather(which * half + part * size, size, sems.at[part])
    gather((1 - which) * half, half, sems.at[parts])
    hold = pltpu.make_async_copy(weight_ref.at[pl.ds(0, held_ref.shape[0])], held_ref, held_sem)
    hold.start()
    ready = [
        functools.partial(wait, which * half + part * size, size, sems.at[part]) for part in range(parts)
    ]
    out_ref[...] = attention(which, length, query_ref, fresh_ref, pages_ref, ready)
    wait((1 - which) * half, half, sems.at[parts])
    hold.wait()


def own_kernel(info_ref, pages_ref, query_ref, fresh_ref, weight_ref, *rest):
    out_ref, held_ref, held_sem = rest
    slots = pages_ref.shape[0]
    count = held_ref.shape[0]
    hold = pltpu.make_async_copy(
        weight_ref.at[pl.ds(weight_ref.shape[0] - count, count)], held_ref, held_sem
    )
    hold.start()
    which = 1 - info_ref[0, slots]
    out_ref[...] = attention(which, info_ref[0, slots + 1], query_ref, fresh_ref, pages_ref, [lambda: None])
    hold.wait()


def attend_cost(slots, rows, page, head):
    return pl.CostEstimate(
        flops=2 * rows * slots * page * head,
        bytes_accessed=4 * slots * page * head,
        transcendentals=rows * slots * page // 2,
    )


def attend_other(info, arrived, queries, fresh, weight, count):
    rows, head = queries.shape[1:]
    slots = info.shape[1] - 128
    page = arrived.shape[1]
    return pl.pallas_call(
        other_kernel,
        out_shape=(
            jax.ShapeDtypeStruct((rows, head), jnp.bfloat16),
            pltpu.VMEM((slots,) + arrived.shape[1:], arrived.dtype),
            pltpu.VMEM((count, weight.shape[1]), weight.dtype),
        ),
        in_specs=[SMEM, HBM, VMEM, VMEM, HBM],
        out_specs=(VMEM, VMEM, VMEM),
        scratch_shapes=[pltpu.SemaphoreType.DMA((3,)), pltpu.SemaphoreType.DMA],
        compiler_params=pltpu.CompilerParams(vmem_limit_bytes=LIMIT),
        cost_estimate=attend_cost(slots, rows, page, head),
        name="attend_other",
    )(info, in_hbm(arrived), queries, fresh, in_hbm(weight))


def attend_own(info, pages, queries, fresh, weight, count):
    rows, head = queries.shape[1:]
    return pl.pallas_call(
        own_kernel,
        out_shape=(
            jax.ShapeDtypeStruct((rows, head), jnp.bfloat16),
            pltpu.VMEM((count, weight.shape[1]), weight.dtype),
        ),
        in_specs=[SMEM, VMEM, VMEM, VMEM, HBM],
        out_specs=(VMEM, VMEM),
        scratch_shapes=[pltpu.SemaphoreType.DMA],
        compiler_params=pltpu.CompilerParams(vmem_limit_bytes=LIMIT),
        cost_estimate=attend_cost(pages.shape[0], rows, pages.shape[1], head),
        name="attend_own",
    )(info, in_vmem(pages), queries, fresh, in_hbm(weight))


def store_kernel(pages_ref, _, moved_ref, sem):
    copy = pltpu.make_async_copy(pages_ref, moved_ref, sem)
    copy.start()
    copy.wait()


def store(pages, after):
    return pl.pallas_call(
        store_kernel,
        out_shape=pltpu.HBM(pages.shape, pages.dtype),
        in_specs=[VMEM, VMEM],
        out_specs=HBM,
        scratch_shapes=[pltpu.SemaphoreType.DMA],
        compiler_params=pltpu.CompilerParams(vmem_limit_bytes=LIMIT),
        cost_estimate=pl.CostEstimate(flops=0, bytes_accessed=2 * pages.size, transcendentals=0),
        name="store_moved",
    )(in_vmem(pages), in_vmem(after))


def project_kernel(kept_ref, partner_ref, first_ref, second_ref, sum_ref, sent_ref):
    steps = sum_ref.shape[0] // 2
    rows = []
    for ref in (kept_ref, partner_ref):
        value = ref[...].astype(jnp.float32)
        rows.append(
            jnp.concatenate([value[at : at + steps] for at in range(0, value.shape[0], steps)], axis=1)
        )
    both = jnp.concatenate(rows, axis=0).astype(jnp.bfloat16)
    tile = 1024
    cut = first_ref.shape[0]
    for at in range(0, first_ref.shape[1], tile):
        product = jnp.dot(both[:, :cut], first_ref[:, at : at + tile], preferred_element_type=jnp.float32)
        product = product + jnp.dot(
            both[:, cut:], second_ref[:, at : at + tile], preferred_element_type=jnp.float32
        )
        sum_ref[:, at : at + tile] = product
        turned = jnp.concatenate([product[steps:], product[:steps]], axis=0)
        sent_ref[:, at : at + tile] = turned.astype(jnp.bfloat16)


def project(kept, partner, first, second, steps):
    wide = first.shape[1]
    return pl.pallas_call(
        project_kernel,
        out_shape=(
            jax.ShapeDtypeStruct((2 * steps, wide), jnp.float32),
            jax.ShapeDtypeStruct((2 * steps, wide), jnp.bfloat16),
        ),
        in_specs=[VMEM, VMEM, VMEM, VMEM],
        out_specs=(VMEM, VMEM),
        compiler_params=pltpu.CompilerParams(vmem_limit_bytes=LIMIT),
        cost_estimate=pl.CostEstimate(
            flops=4 * steps * (first.size + second.size),
            bytes_accessed=2 * (first.size + second.size),
            transcendentals=0,
        ),
        name="project",
    )(kept, partner, in_vmem(first), in_vmem(second))


def on_device(old_cache, old_weight, plan_src, plan_page, lengths, queries, new_kv):
    devices = lax.axis_size("inst") * lax.axis_size("tp")
    steps = queries.shape[1]
    width = old_cache.shape[2]
    heads = new_kv.shape[2] // width
    head = width // 2
    groups = queries.shape[2] // (heads * head)

    tensor = lax.axis_size("tp")
    serving = lax.axis_size("inst")
    pairs = devices // 2
    sides = [[i * tensor + t for i in range(side, serving, 2) for t in range(tensor)] for side in (0, 1)]
    exchange = functools.partial(
        lax.all_to_all, axis_name=BOTH, split_axis=0, concat_axis=0, tiled=True, axis_index_groups=sides
    )
    neighbour_cache = lax.ppermute(old_cache, "inst", [(i, i ^ 1) for i in range(serving)])
    wanted, info, held = make_plan(plan_src, plan_page, lengths[:, :, 0], old_cache, pairs, tensor)
    asked = exchange(wanted)
    taken = take(held, neighbour_cache, asked)
    arrived = exchange(taken.reshape((pairs, 4) + old_cache.shape[1:]))
    arrived = arrived.reshape((pairs * 4,) + old_cache.shape[1:])

    rows = queries.reshape(steps, heads, groups, head).transpose(1, 2, 0, 3)
    rows = rows.reshape(heads, groups * steps, head)
    fresh = new_kv.reshape(steps, heads, width).transpose(1, 0, 2)
    early = old_weight.shape[0] // 4
    passed, pages, first = attend_other(info, arrived, rows, fresh, old_weight, early)
    partner = flipped(passed, 1)
    kept, second = attend_own(info, pages, rows, fresh, old_weight, old_weight.shape[0] - early)

    total, sent = project(kept, partner, first, second, steps)
    moved = store(pages, sent)
    mine = sent[steps:]
    theirs = sent[:steps]
    own = total[:steps]
    own = own + flipped(theirs, 1).astype(jnp.float32) + flipped(theirs, 3).astype(jnp.float32)
    own = own + flipped(mine, 2).astype(jnp.float32)
    own = own + flipped(own.astype(jnp.bfloat16), 4).astype(jnp.float32)
    return own.reshape(1, steps, -1).astype(jnp.bfloat16), moved


def solution(mesh):
    placed = (
        P(BOTH, None, None),
        P("tp", None),
        P(BOTH, None),
        P(BOTH, None),
        P("inst", None, None),
        P(BOTH, None, None),
        P(BOTH, None, None),
    )
    return jax.shard_map(
        on_device,
        mesh=mesh,
        in_specs=placed,
        out_specs=(P(BOTH, None, None), P(BOTH, None, None)),
        check_vma=False,
    )
```

```python
import functools

import jax
import jax.numpy as jnp
from jax import lax
from jax.experimental import pallas as pl
from jax.experimental.pallas import tpu as pltpu
from jax.sharding import PartitionSpec as P

BOTH = ("inst", "tp")
HBM = pl.BlockSpec(memory_space=pltpu.HBM)
VMEM = pl.BlockSpec(memory_space=pltpu.VMEM)
SMEM = pl.BlockSpec(memory_space=pltpu.SMEM)
LIMIT = 6 * 1024 * 1024


def flipped(value, bits):
    size = lax.axis_size("tp")
    return lax.ppermute(value, "tp", [(i, i ^ bits) for i in range(size)])


def in_hbm(value):
    return pltpu.with_memory_space_constraint(value, pltpu.HBM)


def in_vmem(value):
    return pltpu.with_memory_space_constraint(value, pltpu.VMEM)


def plan_kernel(tensor, src_hbm, page_hbm, length_hbm, cache_ref, *rest):
    wanted_ref, place_ref, held_ref, src_ref, page_ref, length_ref, sems = rest
    copies = [
        pltpu.make_async_copy(src_hbm, src_ref, sems.at[0]),
        pltpu.make_async_copy(page_hbm, page_ref, sems.at[1]),
        pltpu.make_async_copy(cache_ref, held_ref, sems.at[2]),
        pltpu.make_async_copy(length_hbm, length_ref, sems.at[3]),
    ]
    for copy in copies:
        copy.start()
    slots = src_ref.shape[1]
    pairs, most = wanted_ref.shape
    side = lax.axis_index("inst") % 2
    shift = tensor.bit_length() - 1
    rows = lax.broadcasted_iota(jnp.int32, (slots, slots), 0)
    columns = lax.broadcasted_iota(jnp.int32, (slots, slots), 1)
    copies[0].wait()
    copies[1].wait()
    src = src_ref[...]
    row_of = lax.shift_right_logical(src, shift)
    pair = lax.shift_left(lax.shift_right_logical(row_of, 1), shift) + (src & (tensor - 1))
    value = page_ref[...] + jnp.where((row_of & 1) == side, 0, cache_ref.shape[0])
    pair_column = jnp.max(jnp.where(rows == columns, pair, 0), axis=1, keepdims=True)
    rank = jnp.sum(jnp.where((pair_column == pair) & (rows < columns), 1, 0), axis=0, keepdims=True)
    named = lax.broadcasted_iota(jnp.int32, (pairs, slots), 0) == pair
    for at in range(most):
        wanted_ref[:, at : at + 1] = jnp.max(
            jnp.where(named & (rank == at), value, -1), axis=1, keepdims=True
        )
    place_ref[:, :slots] = pair * most + rank
    copies[3].wait()
    group = lax.axis_index("tp") % 2
    length = jnp.where(group == 0, length_ref[0, 0], length_ref[0, 1])
    lanes = lax.broadcasted_iota(jnp.int32, (1, place_ref.shape[1] - slots), 1)
    place_ref[:, slots:] = jnp.where(lanes == 0, 1 - group, length)
    copies[2].wait()


def make_plan(plan_src, plan_page, lengths, pages, pairs, tensor):
    slots = plan_src.shape[1]
    return pl.pallas_call(
        functools.partial(plan_kernel, tensor),
        out_shape=(
            jax.ShapeDtypeStruct((pairs, 4), jnp.int32),
            jax.ShapeDtypeStruct((1, slots + 128), jnp.int32),
            pltpu.VMEM(pages.shape, pages.dtype),
        ),
        in_specs=[HBM, HBM, HBM, HBM],
        out_specs=(VMEM, VMEM, VMEM),
        scratch_shapes=[
            pltpu.VMEM((1, slots), jnp.int32),
            pltpu.VMEM((1, slots), jnp.int32),
            pltpu.SMEM(lengths.shape, jnp.int32),
            pltpu.SemaphoreType.DMA((4,)),
        ],
        compiler_params=pltpu.CompilerParams(vmem_limit_bytes=LIMIT),
        name="make_plan",
    )(in_hbm(plan_src), in_hbm(plan_page), in_hbm(lengths), in_hbm(pages))


def take_kernel(asked_ref, own_ref, other_ref, to_ref, turned_ref, at_ref, sem, at_sem):
    count, columns = asked_ref.shape
    pages = own_ref.shape[0]
    shape = (count, turned_ref.shape[1])
    same = lax.broadcasted_iota(jnp.int32, shape, 0) == lax.broadcasted_iota(jnp.int32, shape, 1)
    for column in range(columns):
        turned_ref[column : column + 1, :] = jnp.sum(
            jnp.where(same, asked_ref[:, column : column + 1], 0), axis=0, keepdims=True
        )
    scalars = pltpu.make_async_copy(turned_ref, at_ref, at_sem)
    scalars.start()
    scalars.wait()

    @pl.loop(0, count, init_carry=jnp.int32(0), unroll=2)
    def started(row, total):
        for column in range(columns):
            page = at_ref[column, row]
            to = to_ref.at[row * columns + column]

            @pl.when((page >= 0) & (page < pages))
            def _():
                pltpu.make_async_copy(own_ref.at[page], to, sem).start()

            @pl.when(page >= pages)
            def _():
                pltpu.make_async_copy(other_ref.at[page - pages], to, sem).start()

            total = total + (page >= 0).astype(jnp.int32)
        return total

    @pl.loop(0, started)
    def _(_):
        pltpu.make_async_copy(own_ref.at[0], to_ref.at[0], sem).wait()


def take(own, other, at):
    count = at.shape[0] * at.shape[1]
    shape = (count,) + own.shape[1:]
    turned = (at.shape[1], -(-at.shape[0] // 128) * 128)
    return pl.pallas_call(
        take_kernel,
        out_shape=pltpu.HBM(shape, own.dtype),
        in_specs=[VMEM, VMEM, VMEM],
        out_specs=HBM,
        scratch_shapes=[
            pltpu.VMEM(turned, jnp.int32),
            pltpu.SMEM(turned, jnp.int32),
            pltpu.SemaphoreType.DMA,
            pltpu.SemaphoreType.DMA,
        ],
        compiler_params=pltpu.CompilerParams(vmem_limit_bytes=LIMIT),
        cost_estimate=pl.CostEstimate(
            flops=0, bytes_accessed=count * own.shape[1] * own.shape[2] * 2, transcendentals=0
        ),
        name="take_outgoing",
    )(at, in_vmem(own), in_vmem(other))


def attention(which, length, query_ref, fresh_ref, pages_ref, ready):
    slots, page, width = pages_ref.shape
    head = width // 2
    half = slots // 2
    parts = len(ready)
    size = half // parts
    query = query_ref[which]
    fresh = fresh_ref[which]
    rows = query.shape[0]
    steps = fresh.shape[0]
    scale = head ** (-0.5)
    contract_last = (((1,), (1,)), ((), ()))
    fresh_scores = (
        lax.dot_general(query, fresh[:, :head], contract_last, preferred_element_type=jnp.float32) * scale
    )
    step_of = lax.broadcasted_iota(jnp.int32, (rows, steps), 0) % steps
    key_step = lax.broadcasted_iota(jnp.int32, (rows, steps), 1)
    fresh_scores = jnp.where(step_of >= key_step, fresh_scores, jnp.float32(-1e30))
    highest = jnp.max(fresh_scores, axis=1, keepdims=True)
    scores = []
    for part in range(parts):
        ready[part]()
        keys = pages_ref[pl.ds(which * half + part * size, size), :, :head].reshape(size * page, head)
        found = lax.dot_general(query, keys, contract_last, preferred_element_type=jnp.float32) * scale
        position = lax.broadcasted_iota(jnp.int32, found.shape, 1) + part * size * page
        found = jnp.where(position < length, found, jnp.float32(-1e30))
        highest = jnp.maximum(highest, jnp.max(found, axis=1, keepdims=True))
        scores.append(found)
    fresh_weights = jnp.exp(fresh_scores - highest)
    total = jnp.sum(fresh_weights, axis=1, keepdims=True)
    fresh_values = fresh[:, head:].astype(jnp.float32)
    mixed = jnp.zeros((rows, head), jnp.float32)
    for step in range(steps):
        mixed = mixed + fresh_weights[:, step : step + 1] * fresh_values[step : step + 1, :]
    for part in range(parts):
        weights = jnp.exp(scores[part] - highest)
        total = total + jnp.sum(weights, axis=1, keepdims=True)
        values = pages_ref[pl.ds(which * half + part * size, size), :, head:].reshape(size * page, head)
        mixed = mixed + jnp.dot(weights.astype(jnp.bfloat16), values, preferred_element_type=jnp.float32)
    return (mixed / total).astype(jnp.bfloat16)


def other_kernel(info_ref, arrived_ref, query_ref, fresh_ref, out_ref, pages_ref, sems):
    slots = pages_ref.shape[0]
    half = slots // 2
    parts = sems.shape[0] - 1
    size = half // parts
    which = info_ref[0, slots]
    length = info_ref[0, slots + 1]

    def gather(first, count, sem):
        @pl.loop(0, count, unroll=8)
        def _(at):
            slot = first + at
            pltpu.make_async_copy(arrived_ref.at[info_ref[0, slot]], pages_ref.at[slot], sem).start()

    def wait(first, count, sem):
        block = pages_ref.at[pl.ds(first, count)]
        pltpu.make_async_copy(block, block, sem).wait()

    for part in range(parts):
        gather(which * half + part * size, size, sems.at[part])
    gather((1 - which) * half, half, sems.at[parts])
    ready = [
        functools.partial(wait, which * half + part * size, size, sems.at[part]) for part in range(parts)
    ]
    out_ref[...] = attention(which, length, query_ref, fresh_ref, pages_ref, ready)
    wait((1 - which) * half, half, sems.at[parts])


def own_kernel(info_ref, pages_ref, query_ref, fresh_ref, out_ref):
    slots = pages_ref.shape[0]
    which = 1 - info_ref[0, slots]
    out_ref[...] = attention(which, info_ref[0, slots + 1], query_ref, fresh_ref, pages_ref, [lambda: None])


def attend_cost(slots, rows, page, head):
    return pl.CostEstimate(
        flops=2 * rows * slots * page * head,
        bytes_accessed=4 * slots * page * head,
        transcendentals=rows * slots * page // 2,
    )


def attend_other(info, arrived, queries, fresh):
    rows, head = queries.shape[1:]
    slots = info.shape[1] - 128
    page = arrived.shape[1]
    return pl.pallas_call(
        other_kernel,
        out_shape=(
            jax.ShapeDtypeStruct((rows, head), jnp.bfloat16),
            pltpu.VMEM((slots,) + arrived.shape[1:], arrived.dtype),
        ),
        in_specs=[SMEM, HBM, VMEM, VMEM],
        out_specs=(VMEM, VMEM),
        scratch_shapes=[pltpu.SemaphoreType.DMA((3,))],
        compiler_params=pltpu.CompilerParams(vmem_limit_bytes=LIMIT),
        cost_estimate=attend_cost(slots, rows, page, head),
        name="attend_other",
    )(info, in_hbm(arrived), queries, fresh)


def attend_own(info, pages, queries, fresh):
    rows, head = queries.shape[1:]
    return pl.pallas_call(
        own_kernel,
        out_shape=jax.ShapeDtypeStruct((rows, head), jnp.bfloat16),
        in_specs=[SMEM, VMEM, VMEM, VMEM],
        out_specs=VMEM,
        compiler_params=pltpu.CompilerParams(vmem_limit_bytes=LIMIT),
        cost_estimate=attend_cost(pages.shape[0], rows, pages.shape[1], head),
        name="attend_own",
    )(info, in_vmem(pages), queries, fresh)


def store_kernel(pages_ref, _, moved_ref, sem):
    copy = pltpu.make_async_copy(pages_ref, moved_ref, sem)
    copy.start()
    copy.wait()


def store(pages, after):
    return pl.pallas_call(
        store_kernel,
        out_shape=pltpu.HBM(pages.shape, pages.dtype),
        in_specs=[VMEM, VMEM],
        out_specs=HBM,
        scratch_shapes=[pltpu.SemaphoreType.DMA],
        compiler_params=pltpu.CompilerParams(vmem_limit_bytes=LIMIT),
        cost_estimate=pl.CostEstimate(flops=0, bytes_accessed=2 * pages.size, transcendentals=0),
        name="store_moved",
    )(in_vmem(pages), in_vmem(after))


def project_kernel(kept_ref, partner_ref, weight_ref, sum_ref, sent_ref):
    steps = sum_ref.shape[0] // 2
    rows = []
    for ref in (kept_ref, partner_ref):
        value = ref[...].astype(jnp.float32)
        rows.append(
            jnp.concatenate([value[at : at + steps] for at in range(0, value.shape[0], steps)], axis=1)
        )
    both = jnp.concatenate(rows, axis=0).astype(jnp.bfloat16)
    tile = 1024
    for at in range(0, weight_ref.shape[1], tile):
        product = jnp.dot(both, weight_ref[:, at : at + tile], preferred_element_type=jnp.float32)
        sum_ref[:, at : at + tile] = product
        turned = jnp.concatenate([product[steps:], product[:steps]], axis=0)
        sent_ref[:, at : at + tile] = turned.astype(jnp.bfloat16)


def project(kept, partner, weight, steps):
    wide = weight.shape[1]
    return pl.pallas_call(
        project_kernel,
        out_shape=(
            jax.ShapeDtypeStruct((2 * steps, wide), jnp.float32),
            jax.ShapeDtypeStruct((2 * steps, wide), jnp.bfloat16),
        ),
        in_specs=[VMEM, VMEM, VMEM],
        out_specs=(VMEM, VMEM),
        compiler_params=pltpu.CompilerParams(vmem_limit_bytes=LIMIT),
        cost_estimate=pl.CostEstimate(
            flops=4 * steps * weight.size,
            bytes_accessed=2 * weight.size,
            transcendentals=0,
        ),
        name="project",
    )(kept, partner, in_vmem(weight))


def on_device(old_cache, old_weight, plan_src, plan_page, lengths, queries, new_kv):
    devices = lax.axis_size("inst") * lax.axis_size("tp")
    steps = queries.shape[1]
    width = old_cache.shape[2]
    heads = new_kv.shape[2] // width
    head = width // 2
    groups = queries.shape[2] // (heads * head)

    tensor = lax.axis_size("tp")
    serving = lax.axis_size("inst")
    pairs = devices // 2
    sides = [[i * tensor + t for i in range(side, serving, 2) for t in range(tensor)] for side in (0, 1)]
    exchange = functools.partial(
        lax.all_to_all, axis_name=BOTH, split_axis=0, concat_axis=0, tiled=True, axis_index_groups=sides
    )
    neighbour_cache = lax.ppermute(old_cache, "inst", [(i, i ^ 1) for i in range(serving)])
    wanted, info, held = make_plan(plan_src, plan_page, lengths[:, :, 0], old_cache, pairs, tensor)
    asked = exchange(wanted)
    taken = take(held, neighbour_cache, asked)
    arrived = exchange(taken.reshape((pairs, 4) + old_cache.shape[1:]))
    arrived = arrived.reshape((pairs * 4,) + old_cache.shape[1:])

    rows = queries.reshape(steps, heads, groups, head).transpose(1, 2, 0, 3)
    rows = rows.reshape(heads, groups * steps, head)
    fresh = new_kv.reshape(steps, heads, width).transpose(1, 0, 2)
    passed, pages = attend_other(info, arrived, rows, fresh)
    partner = flipped(passed, 1)
    kept = attend_own(info, pages, rows, fresh)

    total, sent = project(kept, partner, old_weight, steps)
    moved = store(pages, sent)
    mine = sent[steps:]
    theirs = sent[:steps]
    own = total[:steps]
    own = own + flipped(theirs, 1).astype(jnp.float32) + flipped(theirs, 3).astype(jnp.float32)
    own = own + flipped(mine, 2).astype(jnp.float32)
    own = own + flipped(own.astype(jnp.bfloat16), 4).astype(jnp.float32)
    return own.reshape(1, steps, -1).astype(jnp.bfloat16), moved


def solution(mesh):
    placed = (
        P(BOTH, None, None),
        P("tp", None),
        P(BOTH, None),
        P(BOTH, None),
        P("inst", None, None),
        P(BOTH, None, None),
        P(BOTH, None, None),
    )
    return jax.shard_map(
        on_device,
        mesh=mesh,
        in_specs=placed,
        out_specs=(P(BOTH, None, None), P(BOTH, None, None)),
        check_vma=False,
    )
```

```python
import functools

import jax
import jax.numpy as jnp
from jax import lax
from jax.experimental import pallas as pl
from jax.experimental.pallas import tpu as pltpu
from jax.sharding import PartitionSpec as P

BOTH = ("inst", "tp")
HBM = pl.BlockSpec(memory_space=pltpu.HBM)
VMEM = pl.BlockSpec(memory_space=pltpu.VMEM)
SMEM = pl.BlockSpec(memory_space=pltpu.SMEM)
LIMIT = 12 * 1024 * 1024


def flipped(value, bits):
    size = lax.axis_size("tp")
    return lax.ppermute(value, "tp", [(i, i ^ bits) for i in range(size)])


def in_hbm(value):
    return pltpu.with_memory_space_constraint(value, pltpu.HBM)


def in_vmem(value):
    return pltpu.with_memory_space_constraint(value, pltpu.VMEM)


def plan_kernel(tensor, src_hbm, page_hbm, length_hbm, cache_ref, *rest):
    wanted_ref, place_ref, held_ref, src_ref, page_ref, length_ref, sems = rest
    copies = [
        pltpu.make_async_copy(src_hbm, src_ref, sems.at[0]),
        pltpu.make_async_copy(page_hbm, page_ref, sems.at[1]),
        pltpu.make_async_copy(cache_ref, held_ref, sems.at[2]),
        pltpu.make_async_copy(length_hbm, length_ref, sems.at[3]),
    ]
    for copy in copies:
        copy.start()
    slots = src_ref.shape[1]
    pairs, most = wanted_ref.shape
    side = lax.axis_index("inst") % 2
    shift = tensor.bit_length() - 1
    rows = lax.broadcasted_iota(jnp.int32, (slots, slots), 0)
    columns = lax.broadcasted_iota(jnp.int32, (slots, slots), 1)
    copies[0].wait()
    copies[1].wait()
    src = src_ref[...]
    row_of = lax.shift_right_logical(src, shift)
    pair = lax.shift_left(lax.shift_right_logical(row_of, 1), shift) + (src & (tensor - 1))
    value = page_ref[...] + jnp.where((row_of & 1) == side, 0, cache_ref.shape[0])
    pair_column = jnp.max(jnp.where(rows == columns, pair, 0), axis=1, keepdims=True)
    rank = jnp.sum(jnp.where((pair_column == pair) & (rows < columns), 1, 0), axis=0, keepdims=True)
    named = lax.broadcasted_iota(jnp.int32, (pairs, slots), 0) == pair
    for at in range(most):
        wanted_ref[:, at : at + 1] = jnp.max(
            jnp.where(named & (rank == at), value, -1), axis=1, keepdims=True
        )
    place_ref[:, :slots] = pair * most + rank
    copies[3].wait()
    group = lax.axis_index("tp") % 2
    length = jnp.where(group == 0, length_ref[0, 0], length_ref[0, 1])
    lanes = lax.broadcasted_iota(jnp.int32, (1, place_ref.shape[1] - slots), 1)
    place_ref[:, slots:] = jnp.where(lanes == 0, 1 - group, length)
    copies[2].wait()


def make_plan(plan_src, plan_page, lengths, pages, pairs, tensor):
    slots = plan_src.shape[1]
    return pl.pallas_call(
        functools.partial(plan_kernel, tensor),
        out_shape=(
            jax.ShapeDtypeStruct((pairs, 4), jnp.int32),
            jax.ShapeDtypeStruct((1, slots + 128), jnp.int32),
            pltpu.VMEM(pages.shape, pages.dtype),
        ),
        in_specs=[HBM, HBM, HBM, HBM],
        out_specs=(VMEM, VMEM, VMEM),
        scratch_shapes=[
            pltpu.VMEM((1, slots), jnp.int32),
            pltpu.VMEM((1, slots), jnp.int32),
            pltpu.SMEM(lengths.shape, jnp.int32),
            pltpu.SemaphoreType.DMA((4,)),
        ],
        compiler_params=pltpu.CompilerParams(vmem_limit_bytes=LIMIT),
        name="make_plan",
    )(in_hbm(plan_src), in_hbm(plan_page), in_hbm(lengths), in_hbm(pages))


def take_kernel(asked_ref, own_ref, other_ref, to_ref, turned_ref, at_ref, sem, at_sem):
    count, columns = asked_ref.shape
    pages = own_ref.shape[0]
    shape = (count, turned_ref.shape[1])
    same = lax.broadcasted_iota(jnp.int32, shape, 0) == lax.broadcasted_iota(jnp.int32, shape, 1)
    for column in range(columns):
        turned_ref[column : column + 1, :] = jnp.sum(
            jnp.where(same, asked_ref[:, column : column + 1], 0), axis=0, keepdims=True
        )
    scalars = pltpu.make_async_copy(turned_ref, at_ref, at_sem)
    scalars.start()
    scalars.wait()

    @pl.loop(0, count, init_carry=jnp.int32(0), unroll=2)
    def started(row, total):
        for column in range(columns):
            page = at_ref[column, row]
            to = to_ref.at[row * columns + column]

            @pl.when((page >= 0) & (page < pages))
            def _():
                pltpu.make_async_copy(own_ref.at[page], to, sem).start()

            @pl.when(page >= pages)
            def _():
                pltpu.make_async_copy(other_ref.at[page - pages], to, sem).start()

            total = total + (page >= 0).astype(jnp.int32)
        return total

    @pl.loop(0, started)
    def _(_):
        pltpu.make_async_copy(own_ref.at[0], to_ref.at[0], sem).wait()


def take(own, other, at):
    count = at.shape[0] * at.shape[1]
    shape = (count,) + own.shape[1:]
    turned = (at.shape[1], -(-at.shape[0] // 128) * 128)
    return pl.pallas_call(
        take_kernel,
        out_shape=pltpu.HBM(shape, own.dtype),
        in_specs=[VMEM, VMEM, VMEM],
        out_specs=HBM,
        scratch_shapes=[
            pltpu.VMEM(turned, jnp.int32),
            pltpu.SMEM(turned, jnp.int32),
            pltpu.SemaphoreType.DMA,
            pltpu.SemaphoreType.DMA,
        ],
        compiler_params=pltpu.CompilerParams(vmem_limit_bytes=LIMIT),
        cost_estimate=pl.CostEstimate(
            flops=0, bytes_accessed=count * own.shape[1] * own.shape[2] * 2, transcendentals=0
        ),
        name="take_outgoing",
    )(at, in_vmem(own), in_vmem(other))


def attend_kernel(kept, info_ref, arrived_ref, query_ref, fresh_ref, out_ref, pages_ref):
    half, page, width = pages_ref.shape
    head = width // 2
    slots = 2 * half
    which = info_ref[0, slots]
    if kept:
        which = 1 - which
    length = info_ref[0, slots + 1]

    @pl.loop(0, half, unroll=4)
    def _(slot):
        pages_ref[slot] = arrived_ref[info_ref[0, which * half + slot]]

    query = query_ref[which]
    fresh = fresh_ref[which]
    rows = query.shape[0]
    steps = fresh.shape[0]
    scale = head ** (-0.5)
    contract_last = (((1,), (1,)), ((), ()))
    fresh_scores = (
        lax.dot_general(query, fresh[:, :head], contract_last, preferred_element_type=jnp.float32) * scale
    )
    step_of = lax.broadcasted_iota(jnp.int32, (rows, steps), 0) % steps
    key_step = lax.broadcasted_iota(jnp.int32, (rows, steps), 1)
    fresh_scores = jnp.where(step_of >= key_step, fresh_scores, jnp.float32(-1e30))
    keys = pages_ref[:, :, :head].reshape(half * page, head)
    scores = lax.dot_general(query, keys, contract_last, preferred_element_type=jnp.float32) * scale
    position = lax.broadcasted_iota(jnp.int32, scores.shape, 1)
    scores = jnp.where(position < length, scores, jnp.float32(-1e30))
    highest = jnp.maximum(
        jnp.max(scores, axis=1, keepdims=True), jnp.max(fresh_scores, axis=1, keepdims=True)
    )
    fresh_weights = jnp.exp(fresh_scores - highest)
    weights = jnp.exp(scores - highest)
    total = jnp.sum(weights, axis=1, keepdims=True) + jnp.sum(fresh_weights, axis=1, keepdims=True)
    values = pages_ref[:, :, head:].reshape(half * page, head)
    mixed = jnp.dot(weights.astype(jnp.bfloat16), values, preferred_element_type=jnp.float32)
    fresh_values = fresh[:, head:].astype(jnp.float32)
    for step in range(steps):
        mixed = mixed + fresh_weights[:, step : step + 1] * fresh_values[step : step + 1, :]
    out_ref[...] = (mixed / total).astype(jnp.bfloat16)


def attend(kept, info, arrived, queries, fresh, name):
    rows, head = queries.shape[1:]
    half = (info.shape[1] - 128) // 2
    page = arrived.shape[1]
    return pl.pallas_call(
        functools.partial(attend_kernel, kept),
        out_shape=jax.ShapeDtypeStruct((rows, head), jnp.bfloat16),
        in_specs=[SMEM, VMEM, VMEM, VMEM],
        out_specs=VMEM,
        scratch_shapes=[pltpu.VMEM((half,) + arrived.shape[1:], arrived.dtype)],
        compiler_params=pltpu.CompilerParams(vmem_limit_bytes=LIMIT),
        cost_estimate=pl.CostEstimate(
            flops=4 * rows * half * page * head,
            bytes_accessed=4 * half * page * head,
            transcendentals=rows * half * page,
        ),
        name=name,
    )(info, in_vmem(arrived), queries, fresh)


def store_kernel(info_ref, arrived_ref, _, moved_ref, sem):
    @pl.loop(0, moved_ref.shape[0], unroll=4)
    def _(slot):
        pltpu.make_async_copy(arrived_ref.at[info_ref[0, slot]], moved_ref.at[slot], sem).start()

    pltpu.make_async_copy(moved_ref, moved_ref, sem).wait()


def store(info, arrived, after):
    shape = (info.shape[1] - 128,) + arrived.shape[1:]
    return pl.pallas_call(
        store_kernel,
        out_shape=pltpu.HBM(shape, arrived.dtype),
        in_specs=[SMEM, VMEM, VMEM],
        out_specs=HBM,
        scratch_shapes=[pltpu.SemaphoreType.DMA],
        compiler_params=pltpu.CompilerParams(vmem_limit_bytes=LIMIT),
        cost_estimate=pl.CostEstimate(
            flops=0, bytes_accessed=2 * shape[0] * shape[1] * shape[2], transcendentals=0
        ),
        name="store_moved",
    )(info, in_vmem(arrived), in_vmem(after))


def project_kernel(kept_ref, partner_ref, weight_ref, sum_ref, sent_ref):
    steps = sum_ref.shape[0] // 2
    rows = []
    for ref in (kept_ref, partner_ref):
        value = ref[...].astype(jnp.float32)
        rows.append(
            jnp.concatenate([value[at : at + steps] for at in range(0, value.shape[0], steps)], axis=1)
        )
    both = jnp.concatenate(rows, axis=0).astype(jnp.bfloat16)
    tile = 1024
    for at in range(0, weight_ref.shape[1], tile):
        product = jnp.dot(both, weight_ref[:, at : at + tile], preferred_element_type=jnp.float32)
        sum_ref[:, at : at + tile] = product
        turned = jnp.concatenate([product[steps:], product[:steps]], axis=0)
        sent_ref[:, at : at + tile] = turned.astype(jnp.bfloat16)


def project(kept, partner, weight, steps):
    wide = weight.shape[1]
    return pl.pallas_call(
        project_kernel,
        out_shape=(
            jax.ShapeDtypeStruct((2 * steps, wide), jnp.float32),
            jax.ShapeDtypeStruct((2 * steps, wide), jnp.bfloat16),
        ),
        in_specs=[VMEM, VMEM, VMEM],
        out_specs=(VMEM, VMEM),
        compiler_params=pltpu.CompilerParams(vmem_limit_bytes=LIMIT),
        cost_estimate=pl.CostEstimate(
            flops=4 * steps * weight.size,
            bytes_accessed=2 * weight.size,
            transcendentals=0,
        ),
        name="project",
    )(kept, partner, in_vmem(weight))


def on_device(old_cache, old_weight, plan_src, plan_page, lengths, queries, new_kv):
    devices = lax.axis_size("inst") * lax.axis_size("tp")
    steps = queries.shape[1]
    width = old_cache.shape[2]
    heads = new_kv.shape[2] // width
    head = width // 2
    groups = queries.shape[2] // (heads * head)

    tensor = lax.axis_size("tp")
    serving = lax.axis_size("inst")
    pairs = devices // 2
    sides = [[i * tensor + t for i in range(side, serving, 2) for t in range(tensor)] for side in (0, 1)]
    exchange = functools.partial(
        lax.all_to_all, axis_name=BOTH, split_axis=0, concat_axis=0, tiled=True, axis_index_groups=sides
    )
    neighbour_cache = lax.ppermute(old_cache, "inst", [(i, i ^ 1) for i in range(serving)])
    wanted, info, held = make_plan(plan_src, plan_page, lengths[:, :, 0], old_cache, pairs, tensor)
    asked = exchange(wanted)
    taken = take(held, neighbour_cache, asked)
    arrived = exchange(taken.reshape((pairs, 4) + old_cache.shape[1:]))
    arrived = arrived.reshape((pairs * 4,) + old_cache.shape[1:])

    rows = queries.reshape(steps, heads, groups, head).transpose(1, 2, 0, 3)
    rows = rows.reshape(heads, groups * steps, head)
    fresh = new_kv.reshape(steps, heads, width).transpose(1, 0, 2)
    passed = attend(False, info, arrived, rows, fresh, "attend_other")
    partner = flipped(passed, 1)
    kept = attend(True, info, arrived, rows, fresh, "attend_own")

    total, sent = project(kept, partner, old_weight, steps)
    moved = store(info, arrived, sent)
    mine = sent[steps:]
    theirs = sent[:steps]
    own = total[:steps]
    own = own + flipped(theirs, 1).astype(jnp.float32) + flipped(theirs, 3).astype(jnp.float32)
    own = own + flipped(mine, 2).astype(jnp.float32)
    own = own + flipped(own.astype(jnp.bfloat16), 4).astype(jnp.float32)
    return own.reshape(1, steps, -1).astype(jnp.bfloat16), moved


def solution(mesh):
    placed = (
        P(BOTH, None, None),
        P("tp", None),
        P(BOTH, None),
        P(BOTH, None),
        P("inst", None, None),
        P(BOTH, None, None),
        P(BOTH, None, None),
    )
    return jax.shard_map(
        on_device,
        mesh=mesh,
        in_specs=placed,
        out_specs=(P(BOTH, None, None), P(BOTH, None, None)),
        check_vma=False,
    )
```

```python
import functools

import jax
import jax.numpy as jnp
from jax import lax
from jax.experimental import pallas as pl
from jax.experimental.pallas import tpu as pltpu
from jax.sharding import PartitionSpec as P

BOTH = ("inst", "tp")
HBM = pl.BlockSpec(memory_space=pltpu.HBM)
VMEM = pl.BlockSpec(memory_space=pltpu.VMEM)
SMEM = pl.BlockSpec(memory_space=pltpu.SMEM)
LIMIT = 12 * 1024 * 1024


def flipped(value, bits):
    size = lax.axis_size("tp")
    return lax.ppermute(value, "tp", [(i, i ^ bits) for i in range(size)])


def in_hbm(value):
    return pltpu.with_memory_space_constraint(value, pltpu.HBM)


def in_vmem(value):
    return pltpu.with_memory_space_constraint(value, pltpu.VMEM)


def plan_kernel(tensor, src_hbm, page_hbm, length_hbm, cache_ref, *rest):
    wanted_ref, place_ref, held_ref, src_ref, page_ref, length_ref, sems = rest
    copies = [
        pltpu.make_async_copy(src_hbm, src_ref, sems.at[0]),
        pltpu.make_async_copy(page_hbm, page_ref, sems.at[1]),
        pltpu.make_async_copy(cache_ref, held_ref, sems.at[2]),
        pltpu.make_async_copy(length_hbm, length_ref, sems.at[3]),
    ]
    for copy in copies:
        copy.start()
    slots = src_ref.shape[1]
    pairs, most = wanted_ref.shape
    side = lax.axis_index("inst") % 2
    shift = tensor.bit_length() - 1
    rows = lax.broadcasted_iota(jnp.int32, (slots, slots), 0)
    columns = lax.broadcasted_iota(jnp.int32, (slots, slots), 1)
    copies[0].wait()
    copies[1].wait()
    src = src_ref[...]
    row_of = lax.shift_right_logical(src, shift)
    pair = lax.shift_left(lax.shift_right_logical(row_of, 1), shift) + (src & (tensor - 1))
    value = page_ref[...] + jnp.where((row_of & 1) == side, 0, cache_ref.shape[0])
    pair_column = jnp.max(jnp.where(rows == columns, pair, 0), axis=1, keepdims=True)
    rank = jnp.sum(jnp.where((pair_column == pair) & (rows < columns), 1, 0), axis=0, keepdims=True)
    named = lax.broadcasted_iota(jnp.int32, (pairs, slots), 0) == pair
    for at in range(most):
        wanted_ref[:, at : at + 1] = jnp.max(
            jnp.where(named & (rank == at), value, -1), axis=1, keepdims=True
        )
    place_ref[:, :slots] = pair * most + rank
    copies[3].wait()
    group = lax.axis_index("tp") % 2
    length = jnp.where(group == 0, length_ref[0, 0], length_ref[0, 1])
    lanes = lax.broadcasted_iota(jnp.int32, (1, place_ref.shape[1] - slots), 1)
    place_ref[:, slots:] = jnp.where(lanes == 0, 1 - group, length)
    copies[2].wait()


def make_plan(plan_src, plan_page, lengths, pages, pairs, tensor):
    slots = plan_src.shape[1]
    return pl.pallas_call(
        functools.partial(plan_kernel, tensor),
        out_shape=(
            jax.ShapeDtypeStruct((pairs, 4), jnp.int32),
            jax.ShapeDtypeStruct((1, slots + 128), jnp.int32),
            pltpu.VMEM(pages.shape, pages.dtype),
        ),
        in_specs=[HBM, HBM, HBM, HBM],
        out_specs=(VMEM, VMEM, VMEM),
        scratch_shapes=[
            pltpu.VMEM((1, slots), jnp.int32),
            pltpu.VMEM((1, slots), jnp.int32),
            pltpu.SMEM(lengths.shape, jnp.int32),
            pltpu.SemaphoreType.DMA((4,)),
        ],
        compiler_params=pltpu.CompilerParams(vmem_limit_bytes=LIMIT),
        name="make_plan",
    )(in_hbm(plan_src), in_hbm(plan_page), in_hbm(lengths), in_hbm(pages))


def take_kernel(asked_ref, own_ref, other_ref, to_ref, turned_ref, at_ref, at_sem):
    count, columns = asked_ref.shape
    pages = own_ref.shape[0]
    shape = (count, turned_ref.shape[1])
    same = lax.broadcasted_iota(jnp.int32, shape, 0) == lax.broadcasted_iota(jnp.int32, shape, 1)
    for column in range(columns):
        turned_ref[column : column + 1, :] = jnp.sum(
            jnp.where(same, asked_ref[:, column : column + 1], 0), axis=0, keepdims=True
        )
    scalars = pltpu.make_async_copy(turned_ref, at_ref, at_sem)
    scalars.start()
    scalars.wait()

    @pl.loop(0, count, unroll=2)
    def _(row):
        for column in range(columns):
            page = at_ref[column, row]
            within = jnp.maximum(page, 0) & (pages - 1)
            to_ref[row * columns + column] = jnp.where(page >= pages, other_ref[within], own_ref[within])


def take(own, other, at):
    count = at.shape[0] * at.shape[1]
    shape = (count,) + own.shape[1:]
    turned = (at.shape[1], -(-at.shape[0] // 128) * 128)
    return pl.pallas_call(
        take_kernel,
        out_shape=pltpu.VMEM(shape, own.dtype),
        in_specs=[VMEM, VMEM, VMEM],
        out_specs=VMEM,
        scratch_shapes=[
            pltpu.VMEM(turned, jnp.int32),
            pltpu.SMEM(turned, jnp.int32),
            pltpu.SemaphoreType.DMA,
        ],
        compiler_params=pltpu.CompilerParams(vmem_limit_bytes=LIMIT),
        cost_estimate=pl.CostEstimate(
            flops=0, bytes_accessed=count * own.shape[1] * own.shape[2] * 2, transcendentals=0
        ),
        name="take_outgoing",
    )(at, in_vmem(own), in_vmem(other))


def attend_kernel(kept, info_ref, arrived_ref, query_ref, fresh_ref, out_ref, pages_ref):
    half, page, width = pages_ref.shape
    head = width // 2
    slots = 2 * half
    which = info_ref[0, slots]
    if kept:
        which = 1 - which
    length = info_ref[0, slots + 1]

    @pl.loop(0, half, unroll=4)
    def _(slot):
        pages_ref[slot] = arrived_ref[info_ref[0, which * half + slot]]

    query = query_ref[which]
    fresh = fresh_ref[which]
    rows = query.shape[0]
    steps = fresh.shape[0]
    scale = head ** (-0.5)
    contract_last = (((1,), (1,)), ((), ()))
    fresh_scores = (
        lax.dot_general(query, fresh[:, :head], contract_last, preferred_element_type=jnp.float32) * scale
    )
    step_of = lax.broadcasted_iota(jnp.int32, (rows, steps), 0) % steps
    key_step = lax.broadcasted_iota(jnp.int32, (rows, steps), 1)
    fresh_scores = jnp.where(step_of >= key_step, fresh_scores, jnp.float32(-1e30))
    keys = pages_ref[:, :, :head].reshape(half * page, head)
    scores = lax.dot_general(query, keys, contract_last, preferred_element_type=jnp.float32) * scale
    position = lax.broadcasted_iota(jnp.int32, scores.shape, 1)
    scores = jnp.where(position < length, scores, jnp.float32(-1e30))
    highest = jnp.maximum(
        jnp.max(scores, axis=1, keepdims=True), jnp.max(fresh_scores, axis=1, keepdims=True)
    )
    fresh_weights = jnp.exp(fresh_scores - highest)
    weights = jnp.exp(scores - highest)
    total = jnp.sum(weights, axis=1, keepdims=True) + jnp.sum(fresh_weights, axis=1, keepdims=True)
    values = pages_ref[:, :, head:].reshape(half * page, head)
    mixed = jnp.dot(weights.astype(jnp.bfloat16), values, preferred_element_type=jnp.float32)
    fresh_values = fresh[:, head:].astype(jnp.float32)
    for step in range(steps):
        mixed = mixed + fresh_weights[:, step : step + 1] * fresh_values[step : step + 1, :]
    out_ref[...] = (mixed / total).astype(jnp.bfloat16)


def attend(kept, info, arrived, queries, fresh, name):
    rows, head = queries.shape[1:]
    half = (info.shape[1] - 128) // 2
    page = arrived.shape[1]
    return pl.pallas_call(
        functools.partial(attend_kernel, kept),
        out_shape=jax.ShapeDtypeStruct((rows, head), jnp.bfloat16),
        in_specs=[SMEM, VMEM, VMEM, VMEM],
        out_specs=VMEM,
        scratch_shapes=[pltpu.VMEM((half,) + arrived.shape[1:], arrived.dtype)],
        compiler_params=pltpu.CompilerParams(vmem_limit_bytes=LIMIT),
        cost_estimate=pl.CostEstimate(
            flops=4 * rows * half * page * head,
            bytes_accessed=4 * half * page * head,
            transcendentals=rows * half * page,
        ),
        name=name,
    )(info, in_vmem(arrived), queries, fresh)


def store_kernel(info_ref, arrived_ref, _, moved_ref, sem):
    @pl.loop(0, moved_ref.shape[0], unroll=4)
    def _(slot):
        pltpu.make_async_copy(arrived_ref.at[info_ref[0, slot]], moved_ref.at[slot], sem).start()

    pltpu.make_async_copy(moved_ref, moved_ref, sem).wait()


def store(info, arrived, after):
    shape = (info.shape[1] - 128,) + arrived.shape[1:]
    return pl.pallas_call(
        store_kernel,
        out_shape=pltpu.HBM(shape, arrived.dtype),
        in_specs=[SMEM, VMEM, VMEM],
        out_specs=HBM,
        scratch_shapes=[pltpu.SemaphoreType.DMA],
        compiler_params=pltpu.CompilerParams(vmem_limit_bytes=LIMIT),
        cost_estimate=pl.CostEstimate(
            flops=0, bytes_accessed=2 * shape[0] * shape[1] * shape[2], transcendentals=0
        ),
        name="store_moved",
    )(info, in_vmem(arrived), in_vmem(after))


def project_kernel(kept_ref, partner_ref, weight_ref, sum_ref, sent_ref):
    steps = sum_ref.shape[0] // 2
    rows = []
    for ref in (kept_ref, partner_ref):
        value = ref[...].astype(jnp.float32)
        rows.append(
            jnp.concatenate([value[at : at + steps] for at in range(0, value.shape[0], steps)], axis=1)
        )
    both = jnp.concatenate(rows, axis=0).astype(jnp.bfloat16)
    tile = 1024
    for at in range(0, weight_ref.shape[1], tile):
        product = jnp.dot(both, weight_ref[:, at : at + tile], preferred_element_type=jnp.float32)
        sum_ref[:, at : at + tile] = product
        turned = jnp.concatenate([product[steps:], product[:steps]], axis=0)
        sent_ref[:, at : at + tile] = turned.astype(jnp.bfloat16)


def project(kept, partner, weight, steps):
    wide = weight.shape[1]
    return pl.pallas_call(
        project_kernel,
        out_shape=(
            jax.ShapeDtypeStruct((2 * steps, wide), jnp.float32),
            jax.ShapeDtypeStruct((2 * steps, wide), jnp.bfloat16),
        ),
        in_specs=[VMEM, VMEM, VMEM],
        out_specs=(VMEM, VMEM),
        compiler_params=pltpu.CompilerParams(vmem_limit_bytes=LIMIT),
        cost_estimate=pl.CostEstimate(
            flops=4 * steps * weight.size,
            bytes_accessed=2 * weight.size,
            transcendentals=0,
        ),
        name="project",
    )(kept, partner, in_vmem(weight))


def on_device(old_cache, old_weight, plan_src, plan_page, lengths, queries, new_kv):
    devices = lax.axis_size("inst") * lax.axis_size("tp")
    steps = queries.shape[1]
    width = old_cache.shape[2]
    heads = new_kv.shape[2] // width
    head = width // 2
    groups = queries.shape[2] // (heads * head)

    tensor = lax.axis_size("tp")
    serving = lax.axis_size("inst")
    pairs = devices // 2
    sides = [[i * tensor + t for i in range(side, serving, 2) for t in range(tensor)] for side in (0, 1)]
    exchange = functools.partial(
        lax.all_to_all, axis_name=BOTH, split_axis=0, concat_axis=0, tiled=True, axis_index_groups=sides
    )
    neighbour_cache = lax.ppermute(old_cache, "inst", [(i, i ^ 1) for i in range(serving)])
    wanted, info, held = make_plan(plan_src, plan_page, lengths[:, :, 0], old_cache, pairs, tensor)
    asked = exchange(wanted)
    taken = take(held, neighbour_cache, asked)
    arrived = exchange(taken.reshape((pairs, 4) + old_cache.shape[1:]))
    arrived = arrived.reshape((pairs * 4,) + old_cache.shape[1:])

    rows = queries.reshape(steps, heads, groups, head).transpose(1, 2, 0, 3)
    rows = rows.reshape(heads, groups * steps, head)
    fresh = new_kv.reshape(steps, heads, width).transpose(1, 0, 2)
    passed = attend(False, info, arrived, rows, fresh, "attend_other")
    partner = flipped(passed, 1)
    kept = attend(True, info, arrived, rows, fresh, "attend_own")

    total, sent = project(kept, partner, old_weight, steps)
    moved = store(info, arrived, sent)
    mine = sent[steps:]
    theirs = sent[:steps]
    own = total[:steps]
    own = own + flipped(theirs, 1).astype(jnp.float32) + flipped(theirs, 3).astype(jnp.float32)
    own = own + flipped(mine, 2).astype(jnp.float32)
    own = own + flipped(own.astype(jnp.bfloat16), 4).astype(jnp.float32)
    return own.reshape(1, steps, -1).astype(jnp.bfloat16), moved


def solution(mesh):
    placed = (
        P(BOTH, None, None),
        P("tp", None),
        P(BOTH, None),
        P(BOTH, None),
        P("inst", None, None),
        P(BOTH, None, None),
        P(BOTH, None, None),
    )
    return jax.shard_map(
        on_device,
        mesh=mesh,
        in_specs=placed,
        out_specs=(P(BOTH, None, None), P(BOTH, None, None)),
        check_vma=False,
    )
```
